256 devices in a mesh: ctx: 64 (over x, z, core), head: 4 (over y).
Axes of the slice: x: 4, y: 4, z: 8, core: 2. Of those that a mesh axis runs over, the one named last changes fastest.
Arguments:
- queries: bfloat16 [65536, 4096], P(('ctx', 'head')), may hold values from -6 to 6
- key_rows: bfloat16 [65536, 1024], P(('ctx', 'head')), may hold values from -4.5 to 4.5
- value_rows: bfloat16 [65536, 1024], P(('ctx', 'head')), may hold values from -6 to 6
- block_gates: int32 [512, 32, 3], P('ctx', 'head'), may hold values from -1 to 62, as said below
Outputs:
- attended: bfloat16 [65536, 4096], P(('ctx', 'head'))
The draws below stay inside these ranges and needn't reach their ends.
Inputs may be any that keep to these rules, and one draw needn't show every extreme that they name: `block_gates`: entry (t, h, k) is -1 (slot unused) or a block before the block of tile t; the blocks named for one tile and head differ; the entries held by one device (one index of ctx and one of head) name any block at most 2 times, and some block exactly 2 times on every device after the first index of ctx.
All inputs are finite; a program needn't handle non-finite values.
Results may differ from the reference program's by a relative error of at most 0.005.
Values may be sent and summed in bfloat16 or wider, within the bound.
No kernel may reach another device: no remote copies, remote signals or barrier semaphores. Data moves between devices by JAX's collectives and lax.ppermute only.
A program may use at most 128 MiB of HBM per device.

```python
import jax
import jax.numpy as jnp
from jax import lax

HEADS = 32
KV_HEADS = 8
HEAD_DIM = 128
BLOCK = 1024
TILE = 128
TOPK = 3
CAP = 2
BLOCKS = 64
TOKENS = 65536
N_HEAD = 4


def draw_queries(key, part):
    key = jax.random.fold_in(key, 11)
    values_drawn = jnp.clip(jax.random.normal(key, (TOKENS, HEADS, HEAD_DIM), jnp.float32), -4.5, 4.5)
    return values_drawn.reshape(TOKENS, HEADS * HEAD_DIM).astype(jnp.bfloat16)


def draw_key_rows(key, part):
    key = jax.random.fold_in(key, 13)
    values_drawn = jnp.clip(jax.random.normal(key, (TOKENS, KV_HEADS, HEAD_DIM), jnp.float32), -4.5, 4.5)
    return values_drawn.reshape(TOKENS, KV_HEADS * HEAD_DIM).astype(jnp.bfloat16)


def draw_block_gates(key, part):
    key = jax.random.fold_in(key, 17)
    group_heads = HEADS // N_HEAD
    per_block = BLOCK // TILE
    pair_total = per_block * group_heads
    popular_key, device_base = jax.random.split(key)
    popular = jax.random.randint(popular_key, (BLOCKS,), 0, 8) == 0

    def one_device(own_block_id, group_id):
        device_key = jax.random.fold_in(device_base, own_block_id * N_HEAD + group_id)
        jitter_key, drop_key, shuffle_key = jax.random.split(device_key, 3)
        candidates = jnp.arange(BLOCKS, dtype=jnp.int32)
        jitter = jax.random.randint(jitter_key, (BLOCKS,), 0, 2 ** 20)
        ranking = jitter + jnp.where(popular, 2 ** 21, 0) + jnp.where(candidates == own_block_id - 1, 2 ** 22, 0)
        ranking = jnp.where(candidates < own_block_id, ranking, -1)
        ordering = jnp.argsort(-ranking, stable=True).astype(jnp.int32)
        request = jnp.arange(pair_total * TOPK, dtype=jnp.int32)
        entry_slot = request // CAP
        dropped = jnp.logical_and(jax.random.randint(drop_key, (pair_total * TOPK,), 0, 4) == 0, request >= CAP)
        usable = jnp.logical_and(entry_slot < own_block_id, jnp.logical_not(dropped))
        owner_block = jnp.where(usable, ordering[jnp.minimum(entry_slot, BLOCKS - 1)], -1)
        grid_table = owner_block.reshape(TOPK, pair_total)
        shuffle = jax.random.permutation(shuffle_key, pair_total)
        grid_table = grid_table[:, shuffle]
        return grid_table.T.reshape(per_block, group_heads, TOPK)
    block_ids = jnp.repeat(jnp.arange(BLOCKS, dtype=jnp.int32), N_HEAD)
    group_ids = jnp.tile(jnp.arange(N_HEAD, dtype=jnp.int32), BLOCKS)
    tables = jax.vmap(one_device)(block_ids, group_ids)
    tables = tables.reshape(BLOCKS, N_HEAD, per_block, group_heads, TOPK).transpose(0, 2, 1, 3, 4)
    return tables.reshape(BLOCKS * per_block, HEADS, TOPK).astype(jnp.int32)


def block_scale(rng, extent, shards, smallest, largest):
    level, own = 1.0, jax.random.fold_in(rng, 6)
    for dim, parts in shards:
        steps = jnp.exp(jax.random.uniform(jax.random.fold_in(own, dim), (parts,), jnp.float32, smallest / len(shards), largest / len(shards)))
        level = level * jnp.repeat(steps, extent[dim] // parts).reshape([-1 if axis == dim else 1 for axis in range(len(extent))])
    return level


def scatter_about(own_key, extent, scale, bound, cuts=(), kind=jnp.bfloat16):
    drawn = scale * jax.random.normal(own_key, extent, jnp.float32)
    if cuts:
        drawn = drawn * block_scale(own_key, extent, cuts, -0.22, 0.18)
    return jnp.clip(drawn, -bound, bound).astype(kind)


def setup_inputs(seed: int = 0) -> dict:
    splits = jax.random.split(jax.random.key(seed), 5)
    return {
        "queries": draw_queries(jax.random.fold_in(splits[4], 71), 0),
        "key_rows": draw_key_rows(jax.random.fold_in(splits[4], 71), 0),
        "value_rows": scatter_about(splits[2], (TOKENS, KV_HEADS * HEAD_DIM), 1.0, 6.0, ((0, 256),)),
        "block_gates": draw_block_gates(jax.random.fold_in(splits[4], 71), 0),
    }


def reference(queries, key_rows, value_rows, block_gates):
    per_group = HEADS // KV_HEADS
    score_scale = HEAD_DIM ** -0.5
    tiles_per_block = BLOCK // TILE
    query_blocks = queries.reshape(BLOCKS, BLOCK, HEADS, HEAD_DIM)
    key_blocks = key_rows.reshape(BLOCKS, BLOCK, KV_HEADS, HEAD_DIM)
    value_blocks = value_rows.reshape(BLOCKS, BLOCK, KV_HEADS, HEAD_DIM)
    gate_blocks = block_gates.reshape(BLOCKS, tiles_per_block, HEADS, TOPK)
    causal = lax.broadcasted_iota(jnp.int32, (BLOCK, BLOCK), 0) >= lax.broadcasted_iota(jnp.int32, (BLOCK, BLOCK), 1)
    kv_of_head = jnp.arange(HEADS, dtype=jnp.int32) // per_group

    def one_block(inputs):
        query_block, key_block, value_block, gate_block = inputs
        query_wide = query_block.astype(jnp.float32).reshape(BLOCK, KV_HEADS, per_group, HEAD_DIM)
        scores = jnp.einsum("sjgd,kjd->jgsk", query_wide, key_block.astype(jnp.float32)) * score_scale
        scores = jnp.where(causal[None, None], scores, -jnp.inf)
        row_peak = jnp.max(scores, axis=-1, keepdims=True)
        own_log = row_peak + jnp.log(jnp.sum(jnp.exp(scores - row_peak), axis=-1, keepdims=True))
        weights = lax.optimization_barrier(jnp.exp(scores - own_log).astype(jnp.bfloat16)).astype(jnp.float32)
        own_out = jnp.einsum("jgsk,kjd->sjgd", weights, value_block.astype(jnp.float32)).reshape(BLOCK, HEADS, HEAD_DIM)
        own_log = own_log[..., 0].reshape(HEADS, BLOCK)

        def one_tile(tile_inputs):
            tile_query, tile_gate, tile_out, tile_log = tile_inputs
            live_slot = tile_gate >= 0
            chosen = jnp.maximum(tile_gate, 0).astype(jnp.int32)
            gate_keys = key_blocks[chosen, :, kv_of_head[:, None], :].astype(jnp.float32)
            gate_values = value_blocks[chosen, :, kv_of_head[:, None], :].astype(jnp.float32)
            gate_scores = jnp.einsum("shd,hjkd->hjsk", tile_query.astype(jnp.float32), gate_keys) * score_scale
            gate_peak = jnp.max(gate_scores, axis=-1, keepdims=True)
            gate_log = gate_peak + jnp.log(jnp.sum(jnp.exp(gate_scores - gate_peak), axis=-1, keepdims=True))
            gate_weights = lax.optimization_barrier(jnp.exp(gate_scores - gate_log).astype(jnp.bfloat16)).astype(jnp.float32)
            gate_out = jnp.einsum("hjsk,hjkd->shjd", gate_weights, gate_values)
            gate_out = lax.optimization_barrier(gate_out.astype(jnp.bfloat16)).astype(jnp.float32)
            gate_log = gate_log[..., 0]
            live_grid = live_slot[:, :, None]
            top_log = jnp.maximum(tile_log, jnp.max(jnp.where(live_grid, gate_log, tile_log[:, None, :]), axis=1))
            own_weight = jnp.exp(tile_log - top_log)
            gate_weight = jnp.where(live_grid, jnp.exp(gate_log - top_log[:, None, :]), 0.0)
            total_weight = own_weight + jnp.sum(gate_weight, axis=1)
            numerator = own_weight.T[:, :, None] * tile_out + jnp.einsum("hjs,shjd->shd", gate_weight, gate_out)
            return (numerator / total_weight.T[:, :, None]).astype(jnp.bfloat16)

        tiles = lax.map(one_tile, (query_block.reshape(tiles_per_block, TILE, HEADS, HEAD_DIM), gate_block, own_out.reshape(tiles_per_block, TILE, HEADS, HEAD_DIM), own_log.reshape(HEADS, tiles_per_block, TILE).transpose(1, 0, 2)))
        return tiles.reshape(BLOCK, HEADS * HEAD_DIM)

    result = lax.map(one_block, (query_blocks, key_blocks, value_blocks, gate_blocks))
    return result.reshape(TOKENS, HEADS * HEAD_DIM)
```

```python
import math

import jax
import jax.numpy as jnp
from jax import lax
from jax.experimental import pallas as pl
from jax.experimental.pallas import tpu as pltpu
from jax.sharding import PartitionSpec as P

HEAD_DIM = 128
TILE = 128
CAP = 2
N_HEAD = 4
ROW = 16
R = TILE
SLOTS = 5
GROUP = 4
EXTRA = 16
SEND = (2 * R + EXTRA, 3 * R + EXTRA)
LOG_AT = 2 * R
FAR = 2 * R + EXTRA
NEAR = EXTRA + R
FIRST = SEND[1]
FAR_AT = FIRST + SEND[0]
NEAR_AT = FAR_AT + FAR
UNUSED = NEAR_AT + NEAR
SCALE = HEAD_DIM**-0.5
SCALE2 = SCALE * math.log2(math.e)
NEG = -1e30
F32 = jnp.float32
BF16 = jnp.bfloat16
I32 = jnp.int32

SMEM = pl.BlockSpec(memory_space=pltpu.SMEM)
VMEM = pl.BlockSpec(memory_space=pltpu.VMEM)
HBM = pl.BlockSpec(memory_space=pltpu.HBM)


def params(mib):
    return pltpu.CompilerParams(vmem_limit_bytes=mib * 2**20)


def cost(flops, data, exps=0):
    return pl.CostEstimate(flops=flops, bytes_accessed=data, transcendentals=exps)


def shaped(shape, kind=BF16):
    return jax.ShapeDtypeStruct(shape, kind)


def run_copies(pairs, sems):
    copies = [pltpu.make_async_copy(a, b, sems.at[i]) for i, (a, b) in enumerate(pairs)]
    for copy in copies:
        copy.start()
    return copies


def plan_kernel(gates, table, place):
    def clear(i, _):
        table[2 * i] = -1
        table[2 * i + 1] = -1
        return 0

    def note(e, _):
        b = gates[e]
        place[e] = -1

        @pl.when(b >= 0)
        def _():
            at = 2 * b + (table[2 * b] >= 0).astype(I32)
            table[at] = e
            place[e] = at

        return 0

    lax.fori_loop(0, table.shape[0] // 2, clear, 0)
    lax.fori_loop(0, gates.shape[0], note, 0)


def plan(gates, blocks):
    return pl.pallas_call(
        plan_kernel,
        out_shape=(shaped((blocks * CAP,), I32), shaped(gates.shape, I32)),
        in_specs=[SMEM],
        out_specs=(SMEM, SMEM),
        compiler_params=params(4),
        name="plan",
    )(gates)


def split_body(meta, ins, outs, sems):
    pairs = []
    for step in range(N_HEAD):
        g = lax.rem(meta[1] + step, N_HEAD)
        at = 0
        for ref in ins:
            wide = ref.shape[1] // N_HEAD
            cols = pl.ds(pl.multiple_of(g * wide, 128), wide)
            pairs.append((ref.at[:, cols], outs[step].at[:, pl.ds(at, wide)]))
            at += wide
    for copy in run_copies(pairs, sems):
        copy.wait()


def split(meta, ins, *earlier):
    rows, wide = ins[0].shape[0], sum(x.shape[1] for x in ins) // N_HEAD

    def kernel(meta, *refs):
        n = len(ins)
        split_body(meta, refs[:n], refs[n + len(earlier) : -1], refs[-1])

    return pl.pallas_call(
        kernel,
        out_shape=[shaped((rows, wide))] * N_HEAD,
        in_specs=[SMEM] + [HBM] * (len(ins) + len(earlier)),
        out_specs=[VMEM] * N_HEAD,
        scratch_shapes=[pltpu.SemaphoreType.DMA((N_HEAD * len(ins),))],
        compiler_params=params(56),
        cost_estimate=cost(0, 4 * rows * wide * N_HEAD),
        name="split",
    )(meta, *ins, *earlier)


def over_head(parts):
    got = [parts[0]]
    for step in range(1, N_HEAD):
        pairs = [(y, (y + step) % N_HEAD) for y in range(N_HEAD)]
        got.append(lax.ppermute(parts[step], "head", pairs))
    return got


def by_source(y, refs, whole):
    size = refs[0].shape[0]
    pairs = []
    for step, ref in enumerate(refs):
        source = lax.rem(y - step + N_HEAD, N_HEAD)
        pairs.append((ref, whole.at[pl.ds(pl.multiple_of(source * size, 16), size)]))
    return pairs


def join_kernel(meta, *refs):
    pieces, whole, sems = refs[:N_HEAD], refs[N_HEAD], refs[N_HEAD + 1]
    for copy in run_copies(by_source(meta[1], pieces, whole), sems):
        copy.wait()


def join(meta, pieces):
    rows, cols = pieces[0].shape
    return pl.pallas_call(
        join_kernel,
        out_shape=shaped((N_HEAD * rows, cols)),
        in_specs=[SMEM] + [HBM] * N_HEAD,
        out_specs=VMEM,
        scratch_shapes=[pltpu.SemaphoreType.DMA((N_HEAD,))],
        compiler_params=params(6),
        cost_estimate=cost(0, 4 * N_HEAD * rows * cols),
        name="join",
    )(meta, *pieces)


def pack_kernel(meta, table, q0, q1, q2, q3, *refs):
    outs, boxes, q_all, sems = refs[:4], refs[4:8], refs[8], refs[9]
    me = meta[0] // ROW
    for copy in run_copies(by_source(meta[1], (q0, q1, q2, q3), q_all), sems):
        copy.wait()
    lane = lax.broadcasted_iota(I32, (EXTRA, 128), 1)

    def entry(j, target, rank):
        return table[2 * (jnp.maximum(target, 0) * ROW + j) + rank]

    def fill(into, j, row, target, rank):
        e = entry(j, target, rank)

        @pl.when(jnp.logical_and(target >= 0, e >= 0))
        def _():
            tile = lax.div(e, 24)
            head = lax.rem(lax.div(e, 3), 8)
            into[j, row : row + R, :] = q_all[
                pl.ds(pl.multiple_of(tile * R, R), R),
                pl.ds(pl.multiple_of(head * HEAD_DIM, HEAD_DIM), HEAD_DIM),
            ]

    def codes(j, *slots):
        marks = jnp.full((EXTRA, 128), -1, I32)
        for slot, target, rank in slots:
            e = entry(j, target, rank)
            kv_head = lax.div(lax.rem(lax.div(e, 3), 8), 4)
            code = jnp.where(jnp.logical_and(target >= 0, e >= 0), kv_head, -1)
            marks = jnp.where(lane == slot, code, marks)
        return marks.astype(F32).astype(BF16)

    z1, z2, far, near = boxes
    split_row = jnp.where(me == 3, 1, me - 1)

    def own_row(j, _):
        fill(z1, j, 0, me, 0)
        fill(z1, j, R, me, 1)
        z1[j, 2 * R :, :] = codes(j, (0, me, 0), (1, me, 1))
        return 0

    def moved(j, _):
        fill(far, j, 0, 0, 0)
        fill(far, j, R, 0, 1)
        far[j, 2 * R :, :] = codes(j, (2, 0, 0), (3, 0, 1))
        fill(near, j, 0, split_row, 1)
        near[j, R:, :] = codes(j, (4, split_row, 1))
        return 0

    def other_rows(j, _):
        fill(z2, j, 0, me - 1, 0)
        fill(z2, j, R, me - 1, 1)
        fill(z2, j, 2 * R, split_row, 0)
        z2[j, 3 * R :, :] = codes(j, (2, me - 1, 0), (3, me - 1, 1), (4, split_row, 0))
        return 0

    saves = []
    for work, group in ((moved, (2, 3)), (own_row, (0,)), (other_rows, (1,))):
        lax.fori_loop(0, ROW, work, 0)
        for i in group:
            saves.append(pltpu.make_async_copy(boxes[i], outs[i], sems.at[N_HEAD + i]))
            saves[-1].start()
    for save in saves:
        save.wait()


def pack(meta, table, q_parts):
    rows, wide = q_parts[0].shape
    sizes = (SEND[0], SEND[1], FAR, NEAR)
    return pl.pallas_call(
        pack_kernel,
        out_shape=[shaped((ROW, size, HEAD_DIM)) for size in sizes],
        in_specs=[SMEM, SMEM] + [HBM] * N_HEAD,
        out_specs=[HBM] * len(sizes),
        scratch_shapes=[pltpu.VMEM((ROW, size, HEAD_DIM), BF16) for size in sizes]
        + [
            pltpu.VMEM((N_HEAD * rows, wide), BF16),
            pltpu.SemaphoreType.DMA((N_HEAD + len(sizes),)),
        ],
        compiler_params=params(56),
        cost_estimate=cost(0, 2 * (N_HEAD * rows * wide + ROW * sum(sizes) * HEAD_DIM)),
        name="pack",
    )(meta, table, *q_parts)


def insert_kernel(meta, z_in, far, near, *refs):
    z, box, marks, sems = refs[-4:]
    me = meta[0] // ROW
    two, four, last = pl.ds(0, 2 * R), pl.ds(2 * R, R), pl.ds(3 * R, EXTRA)
    has_far, has_near = me <= 1, jnp.logical_or(me == 0, me == 2)
    reads = (
        (jnp.logical_not(has_far), z_in.at[:, two], box.at[:, two], sems.at[0]),
        (has_far, far.at[:, two], box.at[:, two], sems.at[0]),
        (jnp.logical_not(has_near), z_in.at[:, four], box.at[:, four], sems.at[1]),
        (has_near, near.at[:, pl.ds(0, R)], box.at[:, four], sems.at[1]),
    )
    for cond, source, target, sem in reads:

        @pl.when(cond)
        def _(source=source, target=target, sem=sem):
            pltpu.make_async_copy(source, target, sem).start()

    loads = [
        pltpu.make_async_copy(source, marks.at[i], sems.at[2 + i])
        for i, source in enumerate(
            (z_in.at[:, last], far.at[:, pl.ds(2 * R, EXTRA)], near.at[:, pl.ds(R, EXTRA)])
        )
    ]
    for load in loads:
        load.start()
    for load in loads:
        load.wait()
    lane = lax.broadcasted_iota(I32, (EXTRA, 128), 1)
    from_far = jnp.logical_and(lane < 4, me <= 1)
    from_near = jnp.logical_and(lane == 4, lax.rem(me, 2) == 0)
    for j in range(ROW):
        mine, theirs, one = (marks[i, j].astype(F32) for i in range(3))
        mine = jnp.where(from_far, theirs, jnp.where(from_near, one, mine))
        box[j, 3 * R :, :] = mine.astype(BF16)
    saves = []
    for i, region in enumerate((two, four, last)):
        if i < 2:
            pltpu.make_async_copy(z_in.at[:, region], box.at[:, region], sems.at[i]).wait()
        saves.append(pltpu.make_async_copy(box.at[:, region], z.at[:, region], sems.at[5 + i]))
        saves[-1].start()
    for save in saves:
        save.wait()


def insert(meta, z, far, near, *earlier):
    return pl.pallas_call(
        insert_kernel,
        out_shape=shaped(z.shape),
        in_specs=[SMEM] + [HBM] * (3 + len(earlier)),
        out_specs=HBM,
        scratch_shapes=[
            pltpu.VMEM(z.shape, BF16),
            pltpu.VMEM((3, ROW, EXTRA, 128), BF16),
            pltpu.SemaphoreType.DMA((8,)),
        ],
        compiler_params=params(8),
        cost_estimate=cost(0, 4 * z.size),
        name="insert",
    )(meta, z, far, near, *earlier)


def cut_kernel(back, far, near, sems):
    pairs = [
        (back.at[:, pl.ds(0, FAR)], far),
        (back.at[:, pl.ds(LOG_AT, NEAR)], near),
    ]
    for copy in run_copies(pairs, sems):
        copy.wait()


def cut(back):
    return pl.pallas_call(
        cut_kernel,
        out_shape=(shaped((ROW, FAR, HEAD_DIM)), shaped((ROW, NEAR, HEAD_DIM))),
        in_specs=[HBM],
        out_specs=(VMEM, VMEM),
        scratch_shapes=[pltpu.SemaphoreType.DMA((2,))],
        compiler_params=params(6),
        cost_estimate=cost(0, 4 * ROW * (FAR + NEAR) * HEAD_DIM),
        name="cut",
    )(back)


def dot_t(a, b):
    return lax.dot_general(a, b, (((1,), (1,)), ((), ())), preferred_element_type=F32)


def dot(a, b):
    return lax.dot_general(a, b, (((1,), (0,)), ((), ())), preferred_element_type=F32)


def to_row(log):
    lane = lax.broadcasted_iota(I32, (R, R), 1)
    row = lax.broadcasted_iota(I32, (R, R), 0)
    wide = jnp.broadcast_to(log, (R, R))
    return jnp.sum(jnp.where(lane == row, wide, 0.0), axis=0, keepdims=True)


def attend(q, keys, values):
    scores = dot_t(q, keys)
    top = jnp.max(scores, axis=-1, keepdims=True)
    weights = jnp.exp2((scores - top) * SCALE2)
    total = jnp.sum(weights, axis=-1, keepdims=True)
    mixed = dot(weights.astype(BF16), values) / total
    return mixed, top * SCALE + jnp.log(total)


def gate_kernel(part, meta, *refs):
    n_kv = 3 if part else 1
    z, kvs, out = refs[0], refs[1 : 1 + n_kv], refs[1 + n_kv]
    kv, logs, codes, lists, counts, marks, sems = refs[2 + n_kv :]
    me = meta[0] // ROW
    copies = run_copies([(kvs[i], kv.at[i]) for i in range(n_kv)], sems)
    for j in range(ROW):
        marks[j : j + 1, :] = z[j, SEND[part] - EXTRA :, :].astype(F32)[:1].astype(I32)
    known = pltpu.make_async_copy(marks, codes, sems.at[n_kv])
    known.start()
    known.wait()
    groups = ((2, 3), (4,)) if part else ((0, 1),)
    for i in range(2 * len(groups)):
        counts[i] = 0

    def scan(j, _):
        for group, slots in enumerate(groups):
            for slot in slots:
                code = codes[j, slot]

                @pl.when(code >= 0)
                def _(group=group, slot=slot, code=code):
                    i = 2 * group + code
                    n = counts[i]
                    lists[i, n] = j * 8 + slot
                    counts[i] = n + 1

        return 0

    lax.fori_loop(0, ROW, scan, 0)
    for copy in copies:
        copy.wait()
    stores = (jnp.where(me == 0, 0, 1), jnp.where(me == 0, 0, jnp.where(me == 3, 2, 1)))
    for i in range(2 * len(groups)):
        store, kv_head = stores[i // 2] if part else 0, i % 2
        count = counts[i]

        def batch(n, _, i=i, store=store, kv_head=kv_head, count=count):
            keys = kv[store, :, kv_head * HEAD_DIM : (kv_head + 1) * HEAD_DIM]
            values = kv[store, :, (2 + kv_head) * HEAD_DIM : (3 + kv_head) * HEAD_DIM]
            where = []
            for u in range(GROUP):
                item = lists[i, jnp.minimum(n * GROUP + u, count - 1)]
                where.append((lax.div(item, 8), lax.rem(item, 8)))
            done = []
            for u in range(0, GROUP, 2):
                q = [
                    z[j, pl.ds(pl.multiple_of((s - 2 * part) * R, R), R), :]
                    for j, s in where[u : u + 2]
                ]
                done.append(attend(jnp.concatenate(q, axis=0), keys, values))
            for u, (j, s) in enumerate(where):
                mixed, log = done[u // 2]
                rows = slice(u % 2 * R, (u % 2 + 1) * R)
                at = (s - 2 * part) * R + jnp.where(s >= 4, EXTRA, 0)
                out[j, pl.ds(pl.multiple_of(at, 16), R), :] = mixed[rows].astype(BF16)
                log = to_row(log[rows])
                high = log.astype(BF16).astype(F32)
                logs[j, pl.ds(s, 1), :] = high
                logs[j, pl.ds(8 + s, 1), :] = log - high
            return 0

        lax.fori_loop(0, lax.div(count + GROUP - 1, GROUP), batch, 0)
    for j in range(ROW):
        out[j, LOG_AT : LOG_AT + EXTRA, :] = logs[j].astype(BF16)


def gate(meta, part, z, kvs, *held):
    keys = kvs[0].shape[0]
    items = ROW * (2 + part)
    n_kv = len(kvs)

    def kernel(*refs):
        ins = 2 + n_kv + len(held)
        gate_kernel(part, *refs[: 2 + n_kv], refs[ins], *refs[ins + 1 + len(held) :])

    return pl.pallas_call(
        kernel,
        out_shape=[shaped((ROW, SEND[part], HEAD_DIM))] + [shaped(x.shape) for x in held],
        in_specs=[SMEM, VMEM] + [HBM] * (n_kv + len(held)),
        out_specs=[VMEM] + [HBM] * len(held),
        input_output_aliases={2 + n_kv + i: 1 + i for i in range(len(held))},
        scratch_shapes=[
            pltpu.VMEM((n_kv,) + kvs[0].shape, BF16),
            pltpu.VMEM((ROW, 16, 128), F32),
            pltpu.SMEM((ROW, 128), I32),
            pltpu.SMEM((4, ROW * CAP), I32),
            pltpu.SMEM((8,), I32),
            pltpu.VMEM((ROW, 128), I32),
            pltpu.SemaphoreType.DMA((n_kv + 1,)),
        ],
        compiler_params=params(56),
        cost_estimate=cost(4 * items * R * keys * HEAD_DIM, 8 * 2**20, items * R * keys),
        name="gate",
    )(meta, z, *kvs, *held)


def own_kernel(meta, q0, q1, q2, q3, kv, out0, out1, log0, log1, q_all, sems):
    for copy in run_copies(by_source(meta[1], (q0, q1, q2, q3), q_all), sems):
        copy.wait()
    tiles = q_all.shape[0] // R
    heads = q_all.shape[1] // HEAD_DIM
    row = lax.rem(lax.broadcasted_iota(I32, (2 * R, TILE), 0), R)
    seen = row >= lax.broadcasted_iota(I32, (2 * R, TILE), 1)
    for tile in range(tiles):
        rows = slice(tile * R, (tile + 1) * R)
        past, now = slice(0, tile * TILE), slice(tile * TILE, (tile + 1) * TILE)
        out, logs = (out0, log0) if tile % 2 == 0 else (out1, log1)
        to = slice(tile // 2 * R, (tile // 2 + 1) * R)
        for pair in range(0, heads, 2):
            kv_head = pair // (heads // 2)
            q = jnp.concatenate(
                [q_all[rows, h * HEAD_DIM : (h + 1) * HEAD_DIM] for h in (pair, pair + 1)], axis=0
            )
            k_col = slice(kv_head * HEAD_DIM, (kv_head + 1) * HEAD_DIM)
            v_col = slice((2 + kv_head) * HEAD_DIM, (3 + kv_head) * HEAD_DIM)
            near = jnp.where(seen, dot_t(q, kv[now, k_col]), NEG)
            top = jnp.max(near, axis=-1, keepdims=True)
            if tile:
                far = dot_t(q, kv[past, k_col])
                top = jnp.maximum(top, jnp.max(far, axis=-1, keepdims=True))
            near = jnp.exp2((near - top) * SCALE2)
            total = jnp.sum(near, axis=-1, keepdims=True)
            mixed = dot(near.astype(BF16), kv[now, v_col])
            if tile:
                far = jnp.exp2((far - top) * SCALE2)
                total = total + jnp.sum(far, axis=-1, keepdims=True)
                mixed = mixed + dot(far.astype(BF16), kv[past, v_col])
            mixed = mixed / total
            log = top * SCALE + jnp.log(total)
            for u in range(2):
                head = pair + u
                out[to, head * HEAD_DIM : (head + 1) * HEAD_DIM] = mixed[u * R : (u + 1) * R]
                at = tile // 2 * heads + head
                logs[at : at + 1, :] = to_row(log[u * R : (u + 1) * R])


def own(meta, q_parts, kv):
    rows, wide = q_parts[0].shape
    rows = N_HEAD * rows
    units = rows * wide // HEAD_DIM
    out, logs = shaped((rows // 2, wide), F32), shaped((units // R // 2, 128), F32)
    return pl.pallas_call(
        own_kernel,
        out_shape=(out, out, logs, logs),
        in_specs=[SMEM] + [HBM] * N_HEAD + [VMEM],
        out_specs=(VMEM, VMEM, VMEM, VMEM),
        scratch_shapes=[pltpu.VMEM((rows, wide), BF16), pltpu.SemaphoreType.DMA((N_HEAD,))],
        compiler_params=params(56),
        cost_estimate=cost(4 * units * 640 * HEAD_DIM, 8 * 2**20, units * 640),
        name="own",
    )(meta, *q_parts, kv)


def merge_kernel(
    half, meta, place, far_back, z_back, farb, nearb, own_ref, own_log,
    o0, o1, o2, o3, items, logs, got, done, sems
):
    me, y = meta[0] // ROW, meta[1]
    copies = run_copies(
        [
            (far_back, items.at[:, pl.ds(0, SEND[1])]),
            (z_back, items.at[:, pl.ds(FIRST, SEND[0])]),
            (farb, items.at[:, pl.ds(FAR_AT, FAR)]),
            (nearb, items.at[:, pl.ds(NEAR_AT, NEAR)]),
        ],
        sems,
    )
    heads = own_ref.shape[1] // HEAD_DIM
    items[0, UNUSED : UNUSED + R, :] = jnp.zeros((R, HEAD_DIM), BF16)
    logs[0, 32:40, :] = jnp.full((8, 128), NEG, F32)
    for copy in copies:
        copy.wait()
    for j in range(ROW):
        for group, at in enumerate((LOG_AT, FIRST + LOG_AT, FAR_AT + LOG_AT, NEAR_AT)):
            halves = items[j, at : at + EXTRA, :].astype(F32)
            logs[j, 8 * group : 8 * group + 8, :] = halves[:8] + halves[8:]

    def each(pair, _):
        rows = pl.ds(pl.multiple_of(pair * R, R), R)
        where = {}
        for head in range(heads):
            for k in range(3):
                at = place[((2 * pair + half) * heads + head) * 3 + k]
                live = at >= 0
                rank = lax.rem(at, 2)
                j = jnp.where(live, lax.rem(lax.div(at, 2), ROW), 0)
                away = me - lax.div(at, 2 * ROW)
                target = me - away
                far = jnp.logical_and(me >= 2, target == 0)
                four = jnp.logical_or(
                    jnp.logical_and(me == 1, away == 1), jnp.logical_and(me == 3, away == 2)
                )
                base = jnp.where(away == 0, FIRST, jnp.where(far, FAR_AT, 0))
                row = base + rank * R
                row = jnp.where(
                    four, EXTRA + jnp.where(rank == 0, LOG_AT, NEAR_AT), row
                )
                row = jnp.where(live, row, UNUSED)
                slot = jnp.where(away == 0, 8, jnp.where(far, 18, 2)) + rank
                slot = jnp.where(four, 4 + 24 * rank, slot)
                slot = jnp.where(live, slot, 32)
                where[head, k] = (j, row)
                got[k * heads + head : k * heads + head + 1, :] = logs[j, pl.ds(slot, 1), :]
        first = own_log[pl.ds(pl.multiple_of(pair * heads, heads), heads), :]
        others = [got[k * heads : (k + 1) * heads, :] for k in range(3)]
        top = first
        for other in others:
            top = jnp.maximum(top, other)
        weights = [jnp.exp(x - top) for x in [first] + others]
        total = weights[0] + weights[1] + weights[2] + weights[3]
        shares = jnp.concatenate([w / total for w in weights], axis=0)
        shares = jnp.transpose(shares)
        for head in range(heads):
            cols = slice(head * HEAD_DIM, (head + 1) * HEAD_DIM)
            mixed = shares[:, head : head + 1] * own_ref[rows, cols]
            for k in range(3):
                j, row = where[head, k]
                item = items[j, pl.ds(pl.multiple_of(row, 16), R), :].astype(F32)
                at = (k + 1) * heads + head
                mixed = mixed + shares[:, at : at + 1] * item
            done[rows, cols] = mixed.astype(BF16)
        return 0

    lax.fori_loop(0, N_HEAD, each, 0)
    pairs = []
    for step, ref in enumerate((o0, o1, o2, o3)):
        target = lax.rem(y + step, N_HEAD)
        pairs.append((done.at[pl.ds(pl.multiple_of(target * R, R), R)], ref))
    for copy in run_copies(pairs, sems):
        copy.wait()


def merge(half, meta, place, backs, own_out, own_log):
    rows, wide = own_out.shape

    def kernel(*refs):
        merge_kernel(half, *refs)

    return pl.pallas_call(
        kernel,
        out_shape=[shaped((R, wide))] * N_HEAD,
        in_specs=[SMEM, SMEM] + [HBM] * 4 + [VMEM] * 2,
        out_specs=[HBM] * N_HEAD,
        scratch_shapes=[
            pltpu.VMEM((ROW, UNUSED + R, HEAD_DIM), BF16),
            pltpu.VMEM((ROW, 40, 128), F32),
            pltpu.VMEM((24, 128), F32),
            pltpu.VMEM((rows, wide), BF16),
            pltpu.SemaphoreType.DMA((5,)),
        ],
        compiler_params=params(20),
        cost_estimate=cost(20 * rows * wide, 8 * 2**20),
        name="merge",
    )(meta, place, *backs, own_out, own_log)


def finish_kernel(meta, *refs):
    parts, out, sems = refs[:-2], refs[-2], refs[-1]
    y = meta[1]
    wide = parts[0].shape[1]
    pairs = []
    for half in range(2):
        for step in range(N_HEAD):
            source = lax.rem(y - step + N_HEAD, N_HEAD)
            cols = pl.ds(pl.multiple_of(source * wide, 128), wide)
            pairs.append((parts[half * N_HEAD + step], out.at[pl.ds(half * R, R), cols]))
    for copy in run_copies(pairs, sems):
        copy.wait()


def finish(meta, parts):
    wide = parts[0].shape[1]
    return pl.pallas_call(
        finish_kernel,
        out_shape=shaped((2 * TILE, N_HEAD * wide)),
        in_specs=[SMEM] + [HBM] * len(parts),
        out_specs=VMEM,
        scratch_shapes=[pltpu.SemaphoreType.DMA((len(parts),))],
        compiler_params=params(8),
        cost_estimate=cost(0, 4 * 2 * TILE * N_HEAD * wide),
        name="finish",
    )(meta, *parts)


def rows_to(pairs):
    return [(a * ROW + j, b * ROW + j) for a, b in pairs for j in range(ROW)]


def over_row(x):
    groups = [[a * ROW + j for j in range(ROW)] for a in range(4)]
    return lax.all_to_all(
        x, "ctx", split_axis=0, concat_axis=0, tiled=True, axis_index_groups=groups
    )


def local(queries, key_rows, value_rows, block_gates):
    meta = jnp.stack([lax.axis_index("ctx"), lax.axis_index("head")]).astype(I32)
    q_parts = over_head(split(meta, (queries,)))
    table, place = plan(block_gates.reshape(-1), lax.axis_size("ctx"))
    first, second, far, near = pack(meta, table, q_parts)
    first = over_row(first)
    far = lax.ppermute(far, "ctx", rows_to([(3, 0), (2, 1)]))
    near = lax.ppermute(near, "ctx", rows_to([(1, 0), (3, 2)]))
    kv = join(meta, over_head(split(meta, (key_rows, value_rows), near)))
    kv_one = lax.ppermute(kv, "ctx", rows_to([(0, 1), (1, 2), (2, 3)]))
    kv_two = lax.ppermute(kv, "ctx", rows_to([(1, 3)]))
    out0, out1, log0, log1 = own(meta, q_parts, kv)
    second = over_row(insert(meta, second, far, near))
    (first,) = gate(meta, 0, first, (kv,))
    second, first = gate(meta, 1, second, (kv, kv_one, kv_two), first)
    second = over_row(second)
    first = over_row(first)
    far, near = cut(second)
    far = lax.ppermute(far, "ctx", rows_to([(0, 3), (1, 2)]))
    near = lax.ppermute(near, "ctx", rows_to([(0, 1), (2, 3)]))
    backs = (second, first, far, near)
    done = []
    for half, owned in enumerate(((out0, log0), (out1, log1))):
        done += over_head(merge(half, meta, place, backs, *owned))
    return finish(meta, done)


def solution(mesh):
    return jax.shard_map(
        local,
        mesh=mesh,
        in_specs=(
            P(("ctx", "head"), None),
            P(("ctx", "head"), None),
            P(("ctx", "head"), None),
            P("ctx", "head", None),
        ),
        out_specs=P(("ctx", "head"), None),
        check_vma=False,
    )
```

```python
import math

import jax
import jax.numpy as jnp
from jax import lax
from jax.experimental import pallas as pl
from jax.experimental.pallas import tpu as pltpu
from jax.sharding import PartitionSpec as P

HEAD_DIM = 128
TILE = 128
CAP = 2
N_HEAD = 4
ROW = 16
R = TILE
SLOTS = 5
GROUP = 4
EXTRA = 16
SEND = (2 * R + EXTRA, 3 * R + EXTRA)
LOG_AT = 2 * R
FAR = 2 * R + EXTRA
NEAR = EXTRA + R
FIRST = SEND[1]
FAR_AT = FIRST + SEND[0]
NEAR_AT = FAR_AT + FAR
UNUSED = NEAR_AT + NEAR
SCALE = HEAD_DIM**-0.5
SCALE2 = SCALE * math.log2(math.e)
NEG = -1e30
F32 = jnp.float32
BF16 = jnp.bfloat16
I32 = jnp.int32

SMEM = pl.BlockSpec(memory_space=pltpu.SMEM)
VMEM = pl.BlockSpec(memory_space=pltpu.VMEM)
HBM = pl.BlockSpec(memory_space=pltpu.HBM)


def params(mib):
    return pltpu.CompilerParams(vmem_limit_bytes=mib * 2**20)


def cost(flops, data, exps=0):
    return pl.CostEstimate(flops=flops, bytes_accessed=data, transcendentals=exps)


def shaped(shape, kind=BF16):
    return jax.ShapeDtypeStruct(shape, kind)


def run_copies(pairs, sems):
    copies = [pltpu.make_async_copy(a, b, sems.at[i]) for i, (a, b) in enumerate(pairs)]
    for copy in copies:
        copy.start()
    return copies


def plan_kernel(meta, gates, table, place):
    me = meta[0] // ROW

    def clear(i, _):
        table[2 * i] = -1
        table[2 * i + 1] = -1
        return 0

    def note(e, _):
        b = gates[e]
        place[e] = UNUSED // 16 * 1024 + 32 * 16

        @pl.when(b >= 0)
        def _():
            rank = (table[2 * b] >= 0).astype(I32)
            table[2 * b + rank] = e
            target = lax.div(b, ROW)
            away = me - target
            far = jnp.logical_and(me >= 2, target == 0)
            four = jnp.logical_or(
                jnp.logical_and(me == 1, away == 1), jnp.logical_and(me == 3, away == 2)
            )
            row = jnp.where(away == 0, FIRST, jnp.where(far, FAR_AT, 0)) + rank * R
            row = jnp.where(four, EXTRA + jnp.where(rank == 0, LOG_AT, NEAR_AT), row)
            slot = jnp.where(away == 0, 8, jnp.where(far, 18, 2)) + rank
            slot = jnp.where(four, 4 + 24 * rank, slot)
            place[e] = lax.div(row, 16) * 1024 + slot * 16 + lax.rem(b, ROW)

        return 0

    lax.fori_loop(0, table.shape[0] // 2, clear, 0)
    lax.fori_loop(0, gates.shape[0], note, 0)


def plan(meta, gates, blocks):
    return pl.pallas_call(
        plan_kernel,
        out_shape=(shaped((blocks * CAP,), I32), shaped(gates.shape, I32)),
        in_specs=[SMEM, SMEM],
        out_specs=(SMEM, SMEM),
        compiler_params=params(4),
        name="plan",
    )(meta, gates)


def split_kernel(count, first, meta, *refs):
    ins, outs = refs[:count], refs[-2 - 2 * (N_HEAD - first) : -2 - (N_HEAD - first)]
    boxes, (reads, saves) = refs[-2 - (N_HEAD - first) : -2], refs[-2:]
    loads = []
    for i, box in enumerate(boxes):
        g = lax.rem(meta[1] + first + i, N_HEAD)
        at, pairs = 0, []
        for ref in ins:
            wide = ref.shape[1] // N_HEAD
            cols = pl.ds(pl.multiple_of(g * wide, 128), wide)
            pairs.append((ref.at[:, cols], box.at[:, pl.ds(at, wide)]))
            at += wide
        loads.append(run_copies(pairs, reads.at[i]))
    done = []
    for i, load in enumerate(loads):
        for copy in load:
            copy.wait()
        done.append(pltpu.make_async_copy(boxes[i], outs[i], saves.at[i]))
        done[-1].start()
    for copy in done:
        copy.wait()


def split(meta, first, ins, *earlier):
    rows, wide = ins[0].shape[0], sum(x.shape[1] for x in ins) // N_HEAD
    parts = N_HEAD - first

    def kernel(*refs):
        split_kernel(len(ins), first, *refs)

    return pl.pallas_call(
        kernel,
        out_shape=[shaped((rows, wide))] * parts,
        in_specs=[SMEM] + [HBM] * (len(ins) + len(earlier)),
        out_specs=[HBM] * parts,
        scratch_shapes=[pltpu.VMEM((rows, wide), BF16)] * parts
        + [
            pltpu.SemaphoreType.DMA((parts, len(ins))),
            pltpu.SemaphoreType.DMA((parts,)),
        ],
        compiler_params=params(8 if earlier else 56),
        cost_estimate=cost(0, 4 * rows * wide * parts),
        name="split",
    )(meta, *ins, *earlier)


def over_head(parts):
    got = [parts[0]]
    for step in range(1, N_HEAD):
        pairs = [(y, (y + step) % N_HEAD) for y in range(N_HEAD)]
        got.append(lax.ppermute(parts[step], "head", pairs))
    return got


def by_source(y, refs, whole):
    size = refs[0].shape[0]
    pairs = []
    if refs[0].shape[1] != whole.shape[1]:
        wide = whole.shape[1]
        own = refs[0].at[:, pl.ds(pl.multiple_of(y * wide, 128), wide)]
        refs = (own,) + tuple(refs[1:])
    for step, ref in enumerate(refs):
        source = lax.rem(y - step + N_HEAD, N_HEAD)
        pairs.append((ref, whole.at[pl.ds(pl.multiple_of(source * size, 16), size)]))
    return pairs


def join_kernel(meta, *refs):
    pieces, whole, sems = refs[:N_HEAD], refs[N_HEAD], refs[N_HEAD + 1]
    for copy in run_copies(by_source(meta[1], pieces, whole), sems):
        copy.wait()


def join(meta, pieces):
    rows, cols = pieces[0].shape
    return pl.pallas_call(
        join_kernel,
        out_shape=shaped((N_HEAD * rows, cols)),
        in_specs=[SMEM] + [HBM] * N_HEAD,
        out_specs=VMEM,
        scratch_shapes=[pltpu.SemaphoreType.DMA((N_HEAD,))],
        compiler_params=params(6),
        cost_estimate=cost(0, 4 * N_HEAD * rows * cols),
        name="join",
    )(meta, *pieces)


def pack_kernel(meta, table, q0, q1, q2, q3, *refs):
    outs, boxes, q_all, sems = refs[:4], refs[4:8], refs[8], refs[9]
    me = meta[0] // ROW
    for copy in run_copies(by_source(meta[1], (q0, q1, q2, q3), q_all), sems):
        copy.wait()
    lane = lax.broadcasted_iota(I32, (EXTRA, 128), 1)

    def entry(j, target, rank):
        return table[2 * (jnp.maximum(target, 0) * ROW + j) + rank]

    def fill(into, j, row, target, rank):
        e = entry(j, target, rank)

        @pl.when(jnp.logical_and(target >= 0, e >= 0))
        def _():
            tile = lax.div(e, 24)
            head = lax.rem(lax.div(e, 3), 8)
            into[j, row : row + R, :] = q_all[
                pl.ds(pl.multiple_of(tile * R, R), R),
                pl.ds(pl.multiple_of(head * HEAD_DIM, HEAD_DIM), HEAD_DIM),
            ]

    def codes(j, *slots):
        marks = jnp.full((EXTRA, 128), -1, I32)
        for slot, target, rank in slots:
            e = entry(j, target, rank)
            kv_head = lax.div(lax.rem(lax.div(e, 3), 8), 4)
            code = jnp.where(jnp.logical_and(target >= 0, e >= 0), kv_head, -1)
            marks = jnp.where(lane == slot, code, marks)
        return marks.astype(F32).astype(BF16)

    z1, z2, far, near = boxes
    split_row = jnp.where(me == 3, 1, me - 1)

    def own_row(j, _):
        fill(z1, j, 0, me, 0)
        fill(z1, j, R, me, 1)
        z1[j, 2 * R :, :] = codes(j, (0, me, 0), (1, me, 1))
        return 0

    def moved(j, _):
        fill(far, j, 0, 0, 0)
        fill(far, j, R, 0, 1)
        far[j, 2 * R :, :] = codes(j, (2, 0, 0), (3, 0, 1))
        fill(near, j, 0, split_row, 1)
        near[j, R:, :] = codes(j, (4, split_row, 1))
        return 0

    def other_rows(j, _):
        fill(z2, j, 0, me - 1, 0)
        fill(z2, j, R, me - 1, 1)
        fill(z2, j, 2 * R, split_row, 0)
        z2[j, 3 * R :, :] = codes(j, (2, me - 1, 0), (3, me - 1, 1), (4, split_row, 0))
        return 0

    saves = []
    for work, group in ((moved, (2, 3)), (own_row, (0,)), (other_rows, (1,))):
        lax.fori_loop(0, ROW, work, 0)
        for i in group:
            saves.append(pltpu.make_async_copy(boxes[i], outs[i], sems.at[N_HEAD + i]))
            saves[-1].start()
    for save in saves:
        save.wait()


def pack(meta, table, q_parts):
    rows, wide = q_parts[1].shape
    sizes = (SEND[0], SEND[1], FAR, NEAR)
    return pl.pallas_call(
        pack_kernel,
        out_shape=[shaped((ROW, size, HEAD_DIM)) for size in sizes],
        in_specs=[SMEM, SMEM] + [HBM] * N_HEAD,
        out_specs=[HBM] * len(sizes),
        scratch_shapes=[pltpu.VMEM((ROW, size, HEAD_DIM), BF16) for size in sizes]
        + [
            pltpu.VMEM((N_HEAD * rows, wide), BF16),
            pltpu.SemaphoreType.DMA((N_HEAD + len(sizes),)),
        ],
        compiler_params=params(56),
        cost_estimate=cost(0, 2 * (N_HEAD * rows * wide + ROW * sum(sizes) * HEAD_DIM)),
        name="pack",
    )(meta, table, *q_parts)


def insert_kernel(meta, z_in, far, near, *refs):
    z, box, marks, sems = refs[-4:]
    me = meta[0] // ROW
    two, four, last = pl.ds(0, 2 * R), pl.ds(2 * R, R), pl.ds(3 * R, EXTRA)
    has_far, has_near = me <= 1, jnp.logical_or(me == 0, me == 2)
    reads = (
        (jnp.logical_not(has_far), z_in.at[:, two], box.at[:, two], sems.at[0]),
        (has_far, far.at[:, two], box.at[:, two], sems.at[0]),
        (jnp.logical_not(has_near), z_in.at[:, four], box.at[:, four], sems.at[1]),
        (has_near, near.at[:, pl.ds(0, R)], box.at[:, four], sems.at[1]),
    )
    for cond, source, target, sem in reads:

        @pl.when(cond)
        def _(source=source, target=target, sem=sem):
            pltpu.make_async_copy(source, target, sem).start()

    loads = [
        pltpu.make_async_copy(source, marks.at[i], sems.at[2 + i])
        for i, source in enumerate(
            (z_in.at[:, last], far.at[:, pl.ds(2 * R, EXTRA)], near.at[:, pl.ds(R, EXTRA)])
        )
    ]
    for load in loads:
        load.start()
    for load in loads:
        load.wait()
    lane = lax.broadcasted_iota(I32, (EXTRA, 128), 1)
    from_far = jnp.logical_and(lane < 4, me <= 1)
    from_near = jnp.logical_and(lane == 4, lax.rem(me, 2) == 0)
    for j in range(ROW):
        mine, theirs, one = (marks[i, j].astype(F32) for i in range(3))
        mine = jnp.where(from_far, theirs, jnp.where(from_near, one, mine))
        box[j, 3 * R :, :] = mine.astype(BF16)
    saves = []
    for i, region in enumerate((two, four, last)):
        if i < 2:
            pltpu.make_async_copy(z_in.at[:, region], box.at[:, region], sems.at[i]).wait()
        saves.append(pltpu.make_async_copy(box.at[:, region], z.at[:, region], sems.at[5 + i]))
        saves[-1].start()
    for save in saves:
        save.wait()


def insert(meta, z, far, near, *earlier):
    return pl.pallas_call(
        insert_kernel,
        out_shape=shaped(z.shape),
        in_specs=[SMEM] + [HBM] * (3 + len(earlier)),
        out_specs=HBM,
        scratch_shapes=[
            pltpu.VMEM(z.shape, BF16),
            pltpu.VMEM((3, ROW, EXTRA, 128), BF16),
            pltpu.SemaphoreType.DMA((8,)),
        ],
        compiler_params=params(8),
        cost_estimate=cost(0, 4 * z.size),
        name="insert",
    )(meta, z, far, near, *earlier)


def cut_kernel(back, far, near, sems):
    pairs = [
        (back.at[:, pl.ds(0, FAR)], far),
        (back.at[:, pl.ds(LOG_AT, NEAR)], near),
    ]
    for copy in run_copies(pairs, sems):
        copy.wait()


def cut(back):
    return pl.pallas_call(
        cut_kernel,
        out_shape=(shaped((ROW, FAR, HEAD_DIM)), shaped((ROW, NEAR, HEAD_DIM))),
        in_specs=[HBM],
        out_specs=(VMEM, VMEM),
        scratch_shapes=[pltpu.SemaphoreType.DMA((2,))],
        compiler_params=params(6),
        cost_estimate=cost(0, 4 * ROW * (FAR + NEAR) * HEAD_DIM),
        name="cut",
    )(back)


def dot_t(a, b):
    return lax.dot_general(a, b, (((1,), (1,)), ((), ())), preferred_element_type=F32)


def dot(a, b):
    return lax.dot_general(a, b, (((1,), (0,)), ((), ())), preferred_element_type=F32)


def to_row(log):
    lane = lax.broadcasted_iota(I32, (R, R), 1)
    row = lax.broadcasted_iota(I32, (R, R), 0)
    wide = jnp.broadcast_to(log, (R, R))
    return jnp.sum(jnp.where(lane == row, wide, 0.0), axis=0, keepdims=True)


def attend(scores, values):
    top = jnp.max(scores, axis=-1, keepdims=True)
    weights = jnp.exp2((scores - top) * SCALE2)
    total = jnp.sum(weights, axis=-1, keepdims=True)
    mixed = dot(weights.astype(BF16), values) / total
    return mixed, top * SCALE + jnp.log(total)


def gate_kernel(part, meta, *refs):
    n_kv = 3 if part else 1
    z_in, kvs, out_ref = refs[0], refs[1 : 1 + n_kv], refs[1 + n_kv]
    z, out, kv, logs, codes, lists, counts, marks, sems, kv_sems, out_sems = refs[2 + n_kv :]
    me = meta[0] // ROW
    groups = ((2, 3), (4,)) if part else ((0, 1),)
    size = SEND[part]
    known = pltpu.make_async_copy(
        z_in.at[:, pl.ds(size - EXTRA, EXTRA)], z.at[:, pl.ds(size - EXTRA, EXTRA)], sems.at[0]
    )
    known.start()
    loads = []
    for group in range(len(groups)):
        rows = pl.ds(2 * R * group, R * len(groups[group]))
        loads.append(pltpu.make_async_copy(z_in.at[:, rows], z.at[:, rows], sems.at[1 + group]))
        loads[-1].start()
        if part:
            stores = (me == 0, me > 0, False) if group == 0 else (
                me == 0, jnp.logical_or(me == 1, me == 2), me == 3
            )
            for i, chosen in enumerate(stores):
                if chosen is not False:

                    @pl.when(chosen)
                    def _(i=i, group=group):
                        pltpu.make_async_copy(kvs[i], kv.at[group], kv_sems.at[group]).start()
        else:
            pltpu.make_async_copy(kvs[0], kv.at[0], kv_sems.at[0]).start()
    known.wait()
    for j in range(ROW):
        marks[j : j + 1, :] = z[j, size - EXTRA :, :].astype(F32)[:1].astype(I32)
    known = pltpu.make_async_copy(marks, codes, sems.at[0])
    known.start()
    known.wait()
    for i in range(2 * len(groups)):
        counts[i] = 0

    def scan(j, _):
        for group, slots in enumerate(groups):
            for slot in slots:
                code = codes[j, slot]

                @pl.when(code >= 0)
                def _(group=group, slot=slot, code=code):
                    i = 2 * group + code
                    n = counts[i]
                    lists[i, n] = j * 8 + slot
                    counts[i] = n + 1

        return 0

    lax.fori_loop(0, ROW, scan, 0)
    saves = []

    def save(first, rows):
        region = pl.ds(first, rows)
        copy = pltpu.make_async_copy(
            out.at[:, region], out_ref.at[:, region], out_sems.at[len(saves)]
        )
        copy.start()
        saves.append(copy)

    for i in range(2 * len(groups)):
        group, kv_head = i // 2, i % 2
        count = counts[i]
        if kv_head == 0:
            loads[group].wait()
            pltpu.make_async_copy(kvs[0], kv.at[group], kv_sems.at[group]).wait()

        def batch(n, _, i=i, group=group, kv_head=kv_head, count=count):
            keys = kv[group, :, kv_head * HEAD_DIM : (kv_head + 1) * HEAD_DIM]
            values = kv[group, :, (2 + kv_head) * HEAD_DIM : (3 + kv_head) * HEAD_DIM]
            where, scores = [], []
            for u in range(GROUP):
                item = lists[i, jnp.minimum(n * GROUP + u, count - 1)]
                where.append((lax.div(item, 8), lax.rem(item, 8)))
            for u in range(0, GROUP, 2):
                q = [
                    z[j, pl.ds(pl.multiple_of((s - 2 * part) * R, R), R), :]
                    for j, s in where[u : u + 2]
                ]
                scores.append(dot_t(jnp.concatenate(q, axis=0), keys))
            done = [attend(x, values) for x in scores]
            for u, (j, s) in enumerate(where):
                mixed, log = done[u // 2]
                rows = slice(u % 2 * R, (u % 2 + 1) * R)
                at = (s - 2 * part) * R + jnp.where(s >= 4, EXTRA, 0)
                out[j, pl.ds(pl.multiple_of(at, 16), R), :] = mixed[rows].astype(BF16)
                log = to_row(log[rows])
                high = log.astype(BF16).astype(F32)
                logs[j, pl.ds(s, 1), :] = high
                logs[j, pl.ds(8 + s, 1), :] = log - high
            return 0

        lax.fori_loop(0, lax.div(count + GROUP - 1, GROUP), batch, 0)
        if i == 1:
            save(0, 2 * R)
    for j in range(ROW):
        out[j, LOG_AT : LOG_AT + EXTRA, :] = logs[j].astype(BF16)
    save(LOG_AT, size - 2 * R)
    for copy in saves:
        copy.wait()


def gate(meta, part, z, kvs, *held):
    keys = kvs[0].shape[0]
    items = ROW * (2 + part)
    n_kv = len(kvs)

    def kernel(*refs):
        ins = 2 + n_kv + len(held)
        gate_kernel(part, *refs[: 2 + n_kv], refs[ins], *refs[ins + 1 + len(held) :])

    return pl.pallas_call(
        kernel,
        out_shape=[shaped((ROW, SEND[part], HEAD_DIM))] + [shaped(x.shape) for x in held],
        in_specs=[SMEM, HBM] + [HBM] * (n_kv + len(held)),
        out_specs=[HBM] * (1 + len(held)),
        input_output_aliases={2 + n_kv + i: 1 + i for i in range(len(held))},
        scratch_shapes=[
            pltpu.VMEM((ROW, SEND[part], HEAD_DIM), BF16),
            pltpu.VMEM((ROW, SEND[part], HEAD_DIM), BF16),
            pltpu.VMEM((1 + part,) + kvs[0].shape, BF16),
            pltpu.VMEM((ROW, 16, 128), F32),
            pltpu.SMEM((ROW, 128), I32),
            pltpu.SMEM((4, ROW * CAP), I32),
            pltpu.SMEM((8,), I32),
            pltpu.VMEM((ROW, 128), I32),
            pltpu.SemaphoreType.DMA((3,)),
            pltpu.SemaphoreType.DMA((2,)),
            pltpu.SemaphoreType.DMA((2,)),
        ],
        compiler_params=params(56),
        cost_estimate=cost(4 * items * R * keys * HEAD_DIM, 8 * 2**20, items * R * keys),
        name="gate",
    )(meta, z, *kvs, *held)


def own_kernel(meta, q0, q1, q2, q3, kv, _, out0, out1, log0, log1, __, q_all, sems):
    for copy in run_copies(by_source(meta[1], (q0, q1, q2, q3), q_all), sems):
        copy.wait()
    tiles = q_all.shape[0] // R
    heads = q_all.shape[1] // HEAD_DIM
    row = lax.rem(lax.broadcasted_iota(I32, (2 * R, TILE), 0), R)
    seen = row >= lax.broadcasted_iota(I32, (2 * R, TILE), 1)
    for tile in range(tiles):
        rows = slice(tile * R, (tile + 1) * R)
        past, now = slice(0, tile * TILE), slice(tile * TILE, (tile + 1) * TILE)
        out, logs = (out0, log0) if tile % 2 == 0 else (out1, log1)
        to = slice(tile // 2 * R, (tile // 2 + 1) * R)
        for pair in range(0, heads, 2):
            kv_head = pair // (heads // 2)
            q = jnp.concatenate(
                [q_all[rows, h * HEAD_DIM : (h + 1) * HEAD_DIM] for h in (pair, pair + 1)], axis=0
            )
            k_col = slice(kv_head * HEAD_DIM, (kv_head + 1) * HEAD_DIM)
            v_col = slice((2 + kv_head) * HEAD_DIM, (3 + kv_head) * HEAD_DIM)
            near = jnp.where(seen, dot_t(q, kv[now, k_col]), NEG)
            top = jnp.max(near, axis=-1, keepdims=True)
            if tile:
                far = dot_t(q, kv[past, k_col])
                top = jnp.maximum(top, jnp.max(far, axis=-1, keepdims=True))
            near = jnp.exp2((near - top) * SCALE2)
            total = jnp.sum(near, axis=-1, keepdims=True)
            mixed = dot(near.astype(BF16), kv[now, v_col])
            if tile:
                far = jnp.exp2((far - top) * SCALE2)
                total = total + jnp.sum(far, axis=-1, keepdims=True)
                mixed = mixed + dot(far.astype(BF16), kv[past, v_col])
            mixed = mixed / total
            log = top * SCALE + jnp.log(total)
            for u in range(2):
                head = pair + u
                out[to, head * HEAD_DIM : (head + 1) * HEAD_DIM] = mixed[u * R : (u + 1) * R]
                at = tile // 2 * heads + head
                logs[at : at + 1, :] = to_row(log[u * R : (u + 1) * R])


def own(meta, q_parts, kv, held):
    rows, wide = q_parts[1].shape
    rows = N_HEAD * rows
    units = rows * wide // HEAD_DIM
    out, logs = shaped((rows // 2, wide), F32), shaped((units // R // 2, 128), F32)
    return pl.pallas_call(
        own_kernel,
        out_shape=(out, out, logs, logs, shaped(held.shape)),
        in_specs=[SMEM] + [HBM] * N_HEAD + [VMEM, HBM],
        out_specs=(VMEM, VMEM, VMEM, VMEM, HBM),
        input_output_aliases={2 + N_HEAD: 4},
        scratch_shapes=[pltpu.VMEM((rows, wide), BF16), pltpu.SemaphoreType.DMA((N_HEAD,))],
        compiler_params=params(56),
        cost_estimate=cost(4 * units * 640 * HEAD_DIM, 8 * 2**20, units * 640),
        name="own",
    )(meta, *q_parts, kv, held)


def merge_kernel(
    half, meta, place, far_back, z_back, farb, nearb, own_ref, own_log,
    o0, o1, o2, o3, items, logs, got, done, sems
):
    y = meta[1]
    copies = run_copies(
        [
            (far_back, items.at[:, pl.ds(0, SEND[1])]),
            (z_back, items.at[:, pl.ds(FIRST, SEND[0])]),
            (farb, items.at[:, pl.ds(FAR_AT, FAR)]),
            (nearb, items.at[:, pl.ds(NEAR_AT, NEAR)]),
        ],
        sems,
    )
    heads = own_ref.shape[1] // HEAD_DIM
    items[0, UNUSED : UNUSED + R, :] = jnp.zeros((R, HEAD_DIM), BF16)
    logs[0, 32:40, :] = jnp.full((8, 128), NEG, F32)
    for copy in copies:
        copy.wait()
    for j in range(ROW):
        for group, at in enumerate((LOG_AT, FIRST + LOG_AT, FAR_AT + LOG_AT, NEAR_AT)):
            halves = items[j, at : at + EXTRA, :].astype(F32)
            logs[j, 8 * group : 8 * group + 8, :] = halves[:8] + halves[8:]

    def each(pair, _):
        rows = pl.ds(pl.multiple_of(pair * R, R), R)
        where = {}
        for head in range(heads):
            for k in range(3):
                at = place[((2 * pair + half) * heads + head) * 3 + k]
                row = lax.shift_right_logical(at, 10) * 16
                slot = jnp.bitwise_and(lax.shift_right_logical(at, 4), 63)
                j = jnp.bitwise_and(at, 15)
                where[head, k] = (j, row)
                got[k * heads + head : k * heads + head + 1, :] = logs[j, pl.ds(slot, 1), :]
        first = own_log[pl.ds(pl.multiple_of(pair * heads, heads), heads), :]
        others = [got[k * heads : (k + 1) * heads, :] for k in range(3)]
        top = first
        for other in others:
            top = jnp.maximum(top, other)
        weights = [jnp.exp(x - top) for x in [first] + others]
        total = weights[0] + weights[1] + weights[2] + weights[3]
        shares = jnp.concatenate([w / total for w in weights], axis=0)
        shares = jnp.transpose(shares)
        for head in range(heads):
            cols = slice(head * HEAD_DIM, (head + 1) * HEAD_DIM)
            mixed = shares[:, head : head + 1] * own_ref[rows, cols]
            for k in range(3):
                j, row = where[head, k]
                item = items[j, pl.ds(pl.multiple_of(row, 16), R), :].astype(F32)
                at = (k + 1) * heads + head
                mixed = mixed + shares[:, at : at + 1] * item
            done[rows, cols] = mixed.astype(BF16)
        return 0

    lax.fori_loop(0, N_HEAD, each, 0)
    pairs = []
    for step, ref in enumerate((o0, o1, o2, o3)):
        target = lax.rem(y + step, N_HEAD)
        pairs.append((done.at[pl.ds(pl.multiple_of(target * R, R), R)], ref))
    for copy in run_copies(pairs, sems):
        copy.wait()


def merge(half, meta, place, backs, own_out, own_log):
    rows, wide = own_out.shape

    def kernel(*refs):
        merge_kernel(half, *refs)

    return pl.pallas_call(
        kernel,
        out_shape=[shaped((R, wide))] * N_HEAD,
        in_specs=[SMEM, SMEM] + [HBM] * 4 + [VMEM] * 2,
        out_specs=[HBM] * N_HEAD,
        scratch_shapes=[
            pltpu.VMEM((ROW, UNUSED + R, HEAD_DIM), BF16),
            pltpu.VMEM((ROW, 40, 128), F32),
            pltpu.VMEM((24, 128), F32),
            pltpu.VMEM((rows, wide), BF16),
            pltpu.SemaphoreType.DMA((5,)),
        ],
        compiler_params=params(20),
        cost_estimate=cost(20 * rows * wide, 8 * 2**20),
        name="merge",
    )(meta, place, *backs, own_out, own_log)


def finish_kernel(meta, *refs):
    parts, out, sems = refs[:-2], refs[-2], refs[-1]
    y = meta[1]
    wide = parts[0].shape[1]
    pairs = []
    for half in range(2):
        for step in range(N_HEAD):
            source = lax.rem(y - step + N_HEAD, N_HEAD)
            cols = pl.ds(pl.multiple_of(source * wide, 128), wide)
            pairs.append((parts[half * N_HEAD + step], out.at[pl.ds(half * R, R), cols]))
    for copy in run_copies(pairs, sems):
        copy.wait()


def finish(meta, parts):
    wide = parts[0].shape[1]
    return pl.pallas_call(
        finish_kernel,
        out_shape=shaped((2 * TILE, N_HEAD * wide)),
        in_specs=[SMEM] + [HBM] * len(parts),
        out_specs=VMEM,
        scratch_shapes=[pltpu.SemaphoreType.DMA((len(parts),))],
        compiler_params=params(8),
        cost_estimate=cost(0, 4 * 2 * TILE * N_HEAD * wide),
        name="finish",
    )(meta, *parts)


def rows_to(pairs):
    return [(a * ROW + j, b * ROW + j) for a, b in pairs for j in range(ROW)]


def over_row(x):
    groups = [[a * ROW + j for j in range(ROW)] for a in range(4)]
    return lax.all_to_all(
        x, "ctx", split_axis=0, concat_axis=0, tiled=True, axis_index_groups=groups
    )


def local(queries, key_rows, value_rows, block_gates):
    meta = jnp.stack([lax.axis_index("ctx"), lax.axis_index("head")]).astype(I32)
    q_parts = over_head([queries, *split(meta, 1, (queries,))])
    table, place = plan(meta, block_gates.reshape(-1), lax.axis_size("ctx"))
    first, second, far, near = pack(meta, table, q_parts)
    first = over_row(first)
    far = lax.ppermute(far, "ctx", rows_to([(3, 0), (2, 1)]))
    near = lax.ppermute(near, "ctx", rows_to([(1, 0), (3, 2)]))
    kv_cut = split(meta, 0, (key_rows, value_rows), near)
    kv = join(meta, over_head(kv_cut))
    kv_one = lax.ppermute(kv, "ctx", rows_to([(0, 1), (1, 2), (2, 3)]))
    kv_two = lax.ppermute(kv, "ctx", rows_to([(1, 3)]))
    second = over_row(insert(meta, second, far, near))
    (first,) = gate(meta, 0, first, (kv,))
    second, first = gate(meta, 1, second, (kv, kv_one, kv_two), first)
    second = over_row(second)
    out0, out1, log0, log1, first = own(meta, q_parts, kv, first)
    first = over_row(first)
    far, near = cut(second)
    far = lax.ppermute(far, "ctx", rows_to([(0, 3), (1, 2)]))
    near = lax.ppermute(near, "ctx", rows_to([(0, 1), (2, 3)]))
    backs = (second, first, far, near)
    done = []
    for half, owned in enumerate(((out0, log0), (out1, log1))):
        done += over_head(merge(half, meta, place, backs, *owned))
    return finish(meta, done)


def solution(mesh):
    return jax.shard_map(
        local,
        mesh=mesh,
        in_specs=(
            P(("ctx", "head"), None),
            P(("ctx", "head"), None),
            P(("ctx", "head"), None),
            P("ctx", "head", None),
        ),
        out_specs=P(("ctx", "head"), None),
        check_vma=False,
    )
```

```python
import math

import jax
import jax.numpy as jnp
from jax import lax
from jax.experimental import pallas as pl
from jax.experimental.pallas import tpu as pltpu
from jax.sharding import PartitionSpec as P

HEAD_DIM = 128
TILE = 128
CAP = 2
N_HEAD = 4
ROW = 16
R = TILE
SLOTS = 5
GROUP = 4
EXTRA = 16
SEND = (2 * R + EXTRA, 3 * R + EXTRA)
LOG_AT = 2 * R
FAR = 2 * R + EXTRA
NEAR = EXTRA + R
FIRST = SEND[1]
FAR_AT = FIRST + SEND[0]
NEAR_AT = FAR_AT + FAR
UNUSED = NEAR_AT + NEAR
SCALE = HEAD_DIM**-0.5
SCALE2 = SCALE * math.log2(math.e)
NEG = -1e30
F32 = jnp.float32
BF16 = jnp.bfloat16
I32 = jnp.int32

SMEM = pl.BlockSpec(memory_space=pltpu.SMEM)
VMEM = pl.BlockSpec(memory_space=pltpu.VMEM)
HBM = pl.BlockSpec(memory_space=pltpu.HBM)


def params(mib):
    return pltpu.CompilerParams(vmem_limit_bytes=mib * 2**20)


def cost(flops, data, exps=0):
    return pl.CostEstimate(flops=flops, bytes_accessed=data, transcendentals=exps)


def shaped(shape, kind=BF16):
    return jax.ShapeDtypeStruct(shape, kind)


def run_copies(pairs, sems):
    copies = [pltpu.make_async_copy(a, b, sems.at[i]) for i, (a, b) in enumerate(pairs)]
    for copy in copies:
        copy.start()
    return copies


def plan_kernel(meta, gates, table, place):
    me = meta[0] // ROW

    def clear(i, _):
        table[2 * i] = -1
        table[2 * i + 1] = -1
        return 0

    def note(pair, k):
        e = 3 * pair + k
        b = gates[e]
        place[e] = UNUSED // 16 * 1024 + 32 * 16

        @pl.when(b >= 0)
        def _():
            rank = (table[2 * b] >= 0).astype(I32)
            table[2 * b + rank] = pair
            target = lax.shift_right_logical(b, 4)
            away = me - target
            far = jnp.logical_and(me >= 2, target == 0)
            four = jnp.logical_or(
                jnp.logical_and(me == 1, away == 1), jnp.logical_and(me == 3, away == 2)
            )
            row = jnp.where(away == 0, FIRST, jnp.where(far, FAR_AT, 0)) + rank * R
            row = jnp.where(four, EXTRA + jnp.where(rank == 0, LOG_AT, NEAR_AT), row)
            slot = jnp.where(away == 0, 8, jnp.where(far, 18, 2)) + rank
            slot = jnp.where(four, 4 + 24 * rank, slot)
            place[e] = row * 64 + slot * 16 + jnp.bitwise_and(b, 15)

    def notes(pair, _):
        for k in range(3):
            note(pair, k)
        return 0

    lax.fori_loop(0, table.shape[0] // 2, clear, 0)
    lax.fori_loop(0, gates.shape[0] // 3, notes, 0)


def plan(meta, gates, blocks):
    return pl.pallas_call(
        plan_kernel,
        out_shape=(shaped((blocks * CAP,), I32), shaped(gates.shape, I32)),
        in_specs=[SMEM, SMEM],
        out_specs=(SMEM, SMEM),
        compiler_params=params(4),
        name="plan",
    )(meta, gates)


def split_kernel(count, first, parts, meta, *refs):
    ins, outs = refs[:count], refs[-2 - 2 * parts : -2 - parts]
    boxes, (reads, saves) = refs[-2 - parts : -2], refs[-2:]
    loads = []
    for i, box in enumerate(boxes):
        g = lax.rem(meta[1] + first + i, N_HEAD)
        at, pairs = 0, []
        for ref in ins:
            wide = ref.shape[1] // N_HEAD
            cols = pl.ds(pl.multiple_of(g * wide, 128), wide)
            pairs.append((ref.at[:, cols], box.at[:, pl.ds(at, wide)]))
            at += wide
        loads.append(run_copies(pairs, reads.at[i]))
    done = []
    for i, load in enumerate(loads):
        for copy in load:
            copy.wait()
        done.append(pltpu.make_async_copy(boxes[i], outs[i], saves.at[i]))
        done[-1].start()
    for copy in done:
        copy.wait()


def split(meta, first, end, ins, *earlier):
    rows, wide = ins[0].shape[0], sum(x.shape[1] for x in ins) // N_HEAD
    parts = end - first

    def kernel(*refs):
        split_kernel(len(ins), first, parts, *refs)

    return pl.pallas_call(
        kernel,
        out_shape=[shaped((rows, wide))] * parts,
        in_specs=[SMEM] + [HBM] * (len(ins) + len(earlier)),
        out_specs=[HBM] * parts,
        scratch_shapes=[pltpu.VMEM((rows, wide), BF16)] * parts
        + [
            pltpu.SemaphoreType.DMA((parts, len(ins))),
            pltpu.SemaphoreType.DMA((parts,)),
        ],
        compiler_params=params(8 if earlier else 56),
        cost_estimate=cost(0, 4 * rows * wide * parts),
        name="split",
    )(meta, *ins, *earlier)


def over_head(parts):
    got = [parts[0]]
    for step in range(1, N_HEAD):
        pairs = [(y, (y + step) % N_HEAD) for y in range(N_HEAD)]
        got.append(lax.ppermute(parts[step], "head", pairs))
    return got


def by_source(y, refs, whole):
    size = refs[0].shape[0]
    pairs = []
    if refs[0].shape[1] != whole.shape[1]:
        wide = whole.shape[1]
        own = refs[0].at[:, pl.ds(pl.multiple_of(y * wide, 128), wide)]
        refs = (own,) + tuple(refs[1:])
    for step, ref in enumerate(refs):
        source = lax.rem(y - step + N_HEAD, N_HEAD)
        pairs.append((ref, whole.at[pl.ds(pl.multiple_of(source * size, 16), size)]))
    return pairs


def join_kernel(meta, *refs):
    pieces, whole, sems = refs[:N_HEAD], refs[N_HEAD], refs[N_HEAD + 1]
    for copy in run_copies(by_source(meta[1], pieces, whole), sems):
        copy.wait()


def join(meta, pieces):
    rows, cols = pieces[0].shape
    return pl.pallas_call(
        join_kernel,
        out_shape=shaped((N_HEAD * rows, cols)),
        in_specs=[SMEM] + [HBM] * N_HEAD,
        out_specs=VMEM,
        scratch_shapes=[pltpu.SemaphoreType.DMA((N_HEAD,))],
        compiler_params=params(6),
        cost_estimate=cost(0, 4 * N_HEAD * rows * cols),
        name="join",
    )(meta, *pieces)


def pack_kernel(late, meta, table, q0, q1, q2, q3, *refs):
    count = (len(refs) - 2) // 2
    outs, boxes, q_all, sems = refs[:count], refs[count : 2 * count], refs[-2], refs[-1]
    me = meta[0] // ROW
    for copy in run_copies(by_source(meta[1], (q0, q1, q2, q3), q_all), sems):
        copy.wait()
    lane = lax.broadcasted_iota(I32, (EXTRA, 128), 1)

    def entry(j, target, rank):
        return table[2 * (jnp.maximum(target, 0) * ROW + j) + rank]

    def fill(into, j, row, target, rank):
        e = jnp.maximum(entry(j, target, rank), 0)
        tile = lax.shift_right_logical(e, 3)
        head = jnp.bitwise_and(e, 7)
        into[j, row : row + R, :] = q_all[
            pl.ds(pl.multiple_of(tile * R, R), R),
            pl.ds(pl.multiple_of(head * HEAD_DIM, HEAD_DIM), HEAD_DIM),
        ]

    def codes(j, *slots):
        marks = jnp.full((EXTRA, 128), -1, I32)
        for slot, target, rank in slots:
            e = entry(j, target, rank)
            kv_head = jnp.bitwise_and(lax.shift_right_logical(e, 2), 1)
            code = jnp.where(jnp.logical_and(target >= 0, e >= 0), kv_head, -1)
            marks = jnp.where(lane == slot, code, marks)
        return marks.astype(F32).astype(BF16)

    split_row = jnp.where(me == 3, 1, me - 1)

    def own_row(j, _):
        z1 = boxes[2]
        fill(z1, j, 0, me, 0)
        fill(z1, j, R, me, 1)
        z1[j, 2 * R :, :] = codes(j, (0, me, 0), (1, me, 1))
        return 0

    def moved(j, _):
        far, near = boxes[:2]
        fill(far, j, 0, 0, 0)
        fill(far, j, R, 0, 1)
        far[j, 2 * R :, :] = codes(j, (2, 0, 0), (3, 0, 1))
        fill(near, j, 0, split_row, 1)
        near[j, R:, :] = codes(j, (4, split_row, 1))
        return 0

    def other_rows(j, _):
        z2 = boxes[0]
        fill(z2, j, 0, me - 1, 0)
        fill(z2, j, R, me - 1, 1)
        fill(z2, j, 2 * R, split_row, 0)
        z2[j, 3 * R :, :] = codes(j, (2, me - 1, 0), (3, me - 1, 1), (4, split_row, 0))
        return 0

    saves = []
    works = ((other_rows, (0,)),) if late else ((moved, (0, 1)), (own_row, (2,)))
    for work, group in works:
        lax.fori_loop(0, ROW, work, 0, unroll=2)
        for i in group:
            saves.append(pltpu.make_async_copy(boxes[i], outs[i], sems.at[N_HEAD + i]))
            saves[-1].start()
    for save in saves:
        save.wait()


def pack(meta, late, table, q_parts):
    rows, wide = q_parts[1].shape
    sizes = (SEND[1],) if late else (FAR, NEAR, SEND[0])

    def kernel(*refs):
        pack_kernel(late, *refs)

    return pl.pallas_call(
        kernel,
        out_shape=[shaped((ROW, size, HEAD_DIM)) for size in sizes],
        in_specs=[SMEM, SMEM] + [HBM] * N_HEAD,
        out_specs=[HBM] * len(sizes),
        scratch_shapes=[pltpu.VMEM((ROW, size, HEAD_DIM), BF16) for size in sizes]
        + [
            pltpu.VMEM((N_HEAD * rows, wide), BF16),
            pltpu.SemaphoreType.DMA((N_HEAD + len(sizes),)),
        ],
        compiler_params=params(8 if late else 56),
        cost_estimate=cost(0, 2 * (N_HEAD * rows * wide + ROW * sum(sizes) * HEAD_DIM)),
        name="pack",
    )(meta, table, *q_parts)


def insert_kernel(meta, z_in, far, near, *refs):
    z, box, marks, sems = refs[-4:]
    me = meta[0] // ROW
    two, four, last = pl.ds(0, 2 * R), pl.ds(2 * R, R), pl.ds(3 * R, EXTRA)
    has_far, has_near = me <= 1, jnp.logical_or(me == 0, me == 2)
    reads = (
        (jnp.logical_not(has_far), z_in.at[:, two], box.at[:, two], sems.at[0]),
        (has_far, far.at[:, two], box.at[:, two], sems.at[0]),
        (jnp.logical_not(has_near), z_in.at[:, four], box.at[:, four], sems.at[1]),
        (has_near, near.at[:, pl.ds(0, R)], box.at[:, four], sems.at[1]),
    )
    for cond, source, target, sem in reads:

        @pl.when(cond)
        def _(source=source, target=target, sem=sem):
            pltpu.make_async_copy(source, target, sem).start()

    loads = [
        pltpu.make_async_copy(source, marks.at[i], sems.at[2 + i])
        for i, source in enumerate(
            (z_in.at[:, last], far.at[:, pl.ds(2 * R, EXTRA)], near.at[:, pl.ds(R, EXTRA)])
        )
    ]
    for load in loads:
        load.start()
    for load in loads:
        load.wait()
    lane = lax.broadcasted_iota(I32, (EXTRA, 128), 1)
    from_far = jnp.logical_and(lane < 4, me <= 1)
    from_near = jnp.logical_and(lane == 4, lax.rem(me, 2) == 0)
    for j in range(ROW):
        mine, theirs, one = (marks[i, j].astype(F32) for i in range(3))
        mine = jnp.where(from_far, theirs, jnp.where(from_near, one, mine))
        box[j, 3 * R :, :] = mine.astype(BF16)
    saves = []
    for i, region in enumerate((two, four, last)):
        if i < 2:
            pltpu.make_async_copy(z_in.at[:, region], box.at[:, region], sems.at[i]).wait()
        saves.append(pltpu.make_async_copy(box.at[:, region], z.at[:, region], sems.at[5 + i]))
        saves[-1].start()
    for save in saves:
        save.wait()


def insert(meta, z, far, near, *earlier):
    return pl.pallas_call(
        insert_kernel,
        out_shape=shaped(z.shape),
        in_specs=[SMEM] + [HBM] * (3 + len(earlier)),
        out_specs=HBM,
        scratch_shapes=[
            pltpu.VMEM(z.shape, BF16),
            pltpu.VMEM((3, ROW, EXTRA, 128), BF16),
            pltpu.SemaphoreType.DMA((8,)),
        ],
        compiler_params=params(8),
        cost_estimate=cost(0, 4 * z.size),
        name="insert",
    )(meta, z, far, near, *earlier)


def cut_kernel(back, far, near, sems):
    pairs = [
        (back.at[:, pl.ds(0, FAR)], far),
        (back.at[:, pl.ds(LOG_AT, NEAR)], near),
    ]
    for copy in run_copies(pairs, sems):
        copy.wait()


def cut(back):
    return pl.pallas_call(
        cut_kernel,
        out_shape=(shaped((ROW, FAR, HEAD_DIM)), shaped((ROW, NEAR, HEAD_DIM))),
        in_specs=[HBM],
        out_specs=(VMEM, VMEM),
        scratch_shapes=[pltpu.SemaphoreType.DMA((2,))],
        compiler_params=params(6),
        cost_estimate=cost(0, 4 * ROW * (FAR + NEAR) * HEAD_DIM),
        name="cut",
    )(back)


def dot_t(a, b):
    return lax.dot_general(a, b, (((1,), (1,)), ((), ())), preferred_element_type=F32)


def dot(a, b):
    return lax.dot_general(a, b, (((1,), (0,)), ((), ())), preferred_element_type=F32)


def to_row(log):
    lane = lax.broadcasted_iota(I32, (R, R), 1)
    row = lax.broadcasted_iota(I32, (R, R), 0)
    wide = jnp.broadcast_to(log, (R, R))
    return jnp.sum(jnp.where(lane == row, wide, 0.0), axis=0, keepdims=True)


def attend(scores, values):
    top = jnp.max(scores, axis=-1, keepdims=True)
    weights = jnp.exp2((scores - top) * SCALE2)
    total = jnp.sum(weights, axis=-1, keepdims=True)
    mixed = dot(weights.astype(BF16), values) / total
    return mixed, top * SCALE + jnp.log(total)


def gate_kernel(part, meta, *refs):
    n_kv = 3 if part else 1
    z_in, kvs, out_ref = refs[0], refs[1 : 1 + n_kv], refs[1 + n_kv]
    z, out, kv, logs, codes, lists, counts, marks, sems, kv_sems, out_sems = refs[2 + n_kv :]
    me = meta[0] // ROW
    groups = ((2, 3), (4,)) if part else ((0, 1),)
    size = SEND[part]
    known = pltpu.make_async_copy(
        z_in.at[:, pl.ds(size - EXTRA, EXTRA)], z.at[:, pl.ds(size - EXTRA, EXTRA)], sems.at[0]
    )
    known.start()
    loads = []
    for group in range(len(groups)):
        rows = pl.ds(2 * R * group, R * len(groups[group]))
        loads.append(pltpu.make_async_copy(z_in.at[:, rows], z.at[:, rows], sems.at[1 + group]))
        loads[-1].start()
        if part:
            stores = (me == 0, me > 0, False) if group == 0 else (
                me == 0, jnp.logical_or(me == 1, me == 2), me == 3
            )
            for i, chosen in enumerate(stores):
                if chosen is not False:

                    @pl.when(chosen)
                    def _(i=i, group=group):
                        pltpu.make_async_copy(kvs[i], kv.at[group], kv_sems.at[group]).start()
        else:
            pltpu.make_async_copy(kvs[0], kv.at[0], kv_sems.at[0]).start()
    known.wait()
    for j in range(ROW):
        marks[j : j + 1, :] = z[j, size - EXTRA :, :].astype(F32)[:1].astype(I32)
    known = pltpu.make_async_copy(marks, codes, sems.at[0])
    known.start()
    known.wait()
    for i in range(2 * len(groups)):
        counts[i] = 0

    def scan(j, _):
        for group, slots in enumerate(groups):
            for slot in slots:
                code = codes[j, slot]

                @pl.when(code >= 0)
                def _(group=group, slot=slot, code=code):
                    i = 2 * group + code
                    n = counts[i]
                    lists[i, n] = j * 8 + slot
                    counts[i] = n + 1

        return 0

    lax.fori_loop(0, ROW, scan, 0)
    saves = []

    def save(first, rows):
        region = pl.ds(first, rows)
        copy = pltpu.make_async_copy(
            out.at[:, region], out_ref.at[:, region], out_sems.at[len(saves)]
        )
        copy.start()
        saves.append(copy)

    for i in range(2 * len(groups)):
        group, kv_head = i // 2, i % 2
        count = counts[i]
        if kv_head == 0:
            loads[group].wait()
            pltpu.make_async_copy(kvs[0], kv.at[group], kv_sems.at[group]).wait()

        def batch(first, width, i=i, group=group, kv_head=kv_head, count=count):
            keys = kv[group, :, kv_head * HEAD_DIM : (kv_head + 1) * HEAD_DIM]
            values = kv[group, :, (2 + kv_head) * HEAD_DIM : (3 + kv_head) * HEAD_DIM]
            where, scores = [], []
            for u in range(width):
                item = lists[i, jnp.minimum(first + u, count - 1)]
                where.append((lax.shift_right_logical(item, 3), jnp.bitwise_and(item, 7)))
            for u in range(0, width, 2):
                q = [
                    z[j, pl.ds(pl.multiple_of((s - 2 * part) * R, R), R), :]
                    for j, s in where[u : u + 2]
                ]
                scores.append(dot_t(jnp.concatenate(q, axis=0), keys))
            done = [attend(x, values) for x in scores]
            for u, (j, s) in enumerate(where):
                mixed, log = done[u // 2]
                rows = slice(u % 2 * R, (u % 2 + 1) * R)
                at = (s - 2 * part) * R + jnp.where(s >= 4, EXTRA, 0)
                out[j, pl.ds(pl.multiple_of(at, 16), R), :] = mixed[rows].astype(BF16)
                log = to_row(log[rows])
                high = log.astype(BF16).astype(F32)
                logs[j, pl.ds(s, 1), :] = high
                logs[j, pl.ds(8 + s, 1), :] = log - high

        def whole(n, _, batch=batch):
            batch(n * GROUP, GROUP)
            return 0

        fours = lax.shift_right_logical(count + 1, 2)
        lax.fori_loop(0, fours, whole, 0)

        @pl.when(count > GROUP * fours)
        def _(batch=batch, fours=fours):
            batch(GROUP * fours, 2)

        if i == 1:
            save(0, 2 * R)
    for j in range(ROW):
        out[j, LOG_AT : LOG_AT + EXTRA, :] = logs[j].astype(BF16)
    save(LOG_AT, size - 2 * R)
    for copy in saves:
        copy.wait()


def gate(meta, part, z, kvs, *held):
    keys = kvs[0].shape[0]
    items = ROW * (2 + part)
    n_kv = len(kvs)

    def kernel(*refs):
        ins = 2 + n_kv + len(held)
        gate_kernel(part, *refs[: 2 + n_kv], refs[ins], *refs[ins + 1 + len(held) :])

    return pl.pallas_call(
        kernel,
        out_shape=[shaped((ROW, SEND[part], HEAD_DIM))] + [shaped(x.shape) for x in held],
        in_specs=[SMEM, HBM] + [HBM] * (n_kv + len(held)),
        out_specs=[HBM] * (1 + len(held)),
        input_output_aliases={2 + n_kv + i: 1 + i for i in range(len(held))},
        scratch_shapes=[
            pltpu.VMEM((ROW, SEND[part], HEAD_DIM), BF16),
            pltpu.VMEM((ROW, SEND[part], HEAD_DIM), BF16),
            pltpu.VMEM((1 + part,) + kvs[0].shape, BF16),
            pltpu.VMEM((ROW, 16, 128), F32),
            pltpu.SMEM((ROW, 128), I32),
            pltpu.SMEM((4, ROW * CAP), I32),
            pltpu.SMEM((8,), I32),
            pltpu.VMEM((ROW, 128), I32),
            pltpu.SemaphoreType.DMA((3,)),
            pltpu.SemaphoreType.DMA((2,)),
            pltpu.SemaphoreType.DMA((2,)),
        ],
        compiler_params=params(56),
        cost_estimate=cost(4 * items * R * keys * HEAD_DIM, 8 * 2**20, items * R * keys),
        name="gate",
    )(meta, z, *kvs, *held)


def own_kernel(meta, q0, q1, q2, q3, kv, _, out0, out1, log0, log1, __, q_all, sems):
    for copy in run_copies(by_source(meta[1], (q0, q1, q2, q3), q_all), sems):
        copy.wait()
    tiles = q_all.shape[0] // R
    heads = q_all.shape[1] // HEAD_DIM
    row = lax.rem(lax.broadcasted_iota(I32, (2 * R, TILE), 0), R)
    seen = row >= lax.broadcasted_iota(I32, (2 * R, TILE), 1)
    for tile in range(tiles):
        rows = slice(tile * R, (tile + 1) * R)
        past, now = slice(0, tile * TILE), slice(tile * TILE, (tile + 1) * TILE)
        out, logs = (out0, log0) if tile % 2 == 0 else (out1, log1)
        to = slice(tile // 2 * R, (tile // 2 + 1) * R)
        for pair in range(0, heads, 2):
            kv_head = pair // (heads // 2)
            q = jnp.concatenate(
                [q_all[rows, h * HEAD_DIM : (h + 1) * HEAD_DIM] for h in (pair, pair + 1)], axis=0
            )
            k_col = slice(kv_head * HEAD_DIM, (kv_head + 1) * HEAD_DIM)
            v_col = slice((2 + kv_head) * HEAD_DIM, (3 + kv_head) * HEAD_DIM)
            near = jnp.where(seen, dot_t(q, kv[now, k_col]), NEG)
            top = jnp.max(near, axis=-1, keepdims=True)
            if tile:
                far = dot_t(q, kv[past, k_col])
                top = jnp.maximum(top, jnp.max(far, axis=-1, keepdims=True))
            near = jnp.exp2((near - top) * SCALE2)
            total = jnp.sum(near, axis=-1, keepdims=True)
            mixed = dot(near.astype(BF16), kv[now, v_col])
            if tile:
                far = jnp.exp2((far - top) * SCALE2)
                total = total + jnp.sum(far, axis=-1, keepdims=True)
                mixed = mixed + dot(far.astype(BF16), kv[past, v_col])
            mixed = mixed / total
            log = top * SCALE + jnp.log(total)
            for u in range(2):
                head = pair + u
                out[to, head * HEAD_DIM : (head + 1) * HEAD_DIM] = mixed[u * R : (u + 1) * R]
                at = tile // 2 * heads + head
                logs[at : at + 1, :] = to_row(log[u * R : (u + 1) * R])


def own(meta, q_parts, kv, held):
    rows, wide = q_parts[1].shape
    rows = N_HEAD * rows
    units = rows * wide // HEAD_DIM
    out, logs = shaped((rows // 2, wide), F32), shaped((units // R // 2, 128), F32)
    return pl.pallas_call(
        own_kernel,
        out_shape=(out, out, logs, logs, shaped(held.shape)),
        in_specs=[SMEM] + [HBM] * N_HEAD + [VMEM, HBM],
        out_specs=(VMEM, VMEM, VMEM, VMEM, HBM),
        input_output_aliases={2 + N_HEAD: 4},
        scratch_shapes=[pltpu.VMEM((rows, wide), BF16), pltpu.SemaphoreType.DMA((N_HEAD,))],
        compiler_params=params(56),
        cost_estimate=cost(4 * units * 640 * HEAD_DIM, 8 * 2**20, units * 640),
        name="own",
    )(meta, *q_parts, kv, held)


def merge_kernel(
    half, meta, place, far_back, z_back, farb, nearb, own_ref, own_log,
    o0, o1, o2, o3, items, logs, got, done, sems
):
    y = meta[1]
    copies = run_copies(
        [
            (far_back, items.at[:, pl.ds(0, SEND[1])]),
            (z_back, items.at[:, pl.ds(FIRST, SEND[0])]),
            (farb, items.at[:, pl.ds(FAR_AT, FAR)]),
            (nearb, items.at[:, pl.ds(NEAR_AT, NEAR)]),
        ],
        sems,
    )
    heads = own_ref.shape[1] // HEAD_DIM
    items[0, UNUSED : UNUSED + R, :] = jnp.zeros((R, HEAD_DIM), BF16)
    logs[0, 32:40, :] = jnp.full((8, 128), NEG, F32)
    for copy in copies:
        copy.wait()
    for j in range(ROW):
        for group, at in enumerate((LOG_AT, FIRST + LOG_AT, FAR_AT + LOG_AT, NEAR_AT)):
            halves = items[j, at : at + EXTRA, :].astype(F32)
            logs[j, 8 * group : 8 * group + 8, :] = halves[:8] + halves[8:]

    def each(pair, _):
        rows = pl.ds(pl.multiple_of(pair * R, R), R)
        where = {}
        for head in range(heads):
            for k in range(3):
                at = place[((2 * pair + half) * heads + head) * 3 + k]
                row = lax.shift_right_logical(at, 10) * 16
                slot = jnp.bitwise_and(lax.shift_right_logical(at, 4), 63)
                j = jnp.bitwise_and(at, 15)
                where[head, k] = (j, row)
                got[k * heads + head : k * heads + head + 1, :] = logs[j, pl.ds(slot, 1), :]
        first = own_log[pl.ds(pl.multiple_of(pair * heads, heads), heads), :]
        others = [got[k * heads : (k + 1) * heads, :] for k in range(3)]
        top = first
        for other in others:
            top = jnp.maximum(top, other)
        weights = [jnp.exp(x - top) for x in [first] + others]
        total = weights[0] + weights[1] + weights[2] + weights[3]
        shares = jnp.concatenate([w / total for w in weights], axis=0)
        shares = jnp.transpose(shares)
        for head in range(heads):
            cols = slice(head * HEAD_DIM, (head + 1) * HEAD_DIM)
            mixed = shares[:, head : head + 1] * own_ref[rows, cols]
            for k in range(3):
                j, row = where[head, k]
                item = items[j, pl.ds(pl.multiple_of(row, 16), R), :].astype(F32)
                at = (k + 1) * heads + head
                mixed = mixed + shares[:, at : at + 1] * item
            done[rows, cols] = mixed.astype(BF16)
        return 0

    lax.fori_loop(0, N_HEAD, each, 0)
    pairs = []
    for step, ref in enumerate((o0, o1, o2, o3)):
        target = lax.rem(y + step, N_HEAD)
        pairs.append((done.at[pl.ds(pl.multiple_of(target * R, R), R)], ref))
    for copy in run_copies(pairs, sems):
        copy.wait()


def merge(half, meta, place, backs, own_out, own_log):
    rows, wide = own_out.shape

    def kernel(*refs):
        merge_kernel(half, *refs)

    return pl.pallas_call(
        kernel,
        out_shape=[shaped((R, wide))] * N_HEAD,
        in_specs=[SMEM, SMEM] + [HBM] * 4 + [VMEM] * 2,
        out_specs=[HBM] * N_HEAD,
        scratch_shapes=[
            pltpu.VMEM((ROW, UNUSED + R, HEAD_DIM), BF16),
            pltpu.VMEM((ROW, 40, 128), F32),
            pltpu.VMEM((24, 128), F32),
            pltpu.VMEM((rows, wide), BF16),
            pltpu.SemaphoreType.DMA((5,)),
        ],
        compiler_params=params(20),
        cost_estimate=cost(20 * rows * wide, 8 * 2**20),
        name="merge",
    )(meta, place, *backs, own_out, own_log)


def finish_kernel(meta, *refs):
    parts, out, sems = refs[:-2], refs[-2], refs[-1]
    y = meta[1]
    wide = parts[0].shape[1]
    pairs = []
    for half in range(2):
        for step in range(N_HEAD):
            source = lax.rem(y - step + N_HEAD, N_HEAD)
            cols = pl.ds(pl.multiple_of(source * wide, 128), wide)
            pairs.append((parts[half * N_HEAD + step], out.at[pl.ds(half * R, R), cols]))
    for copy in run_copies(pairs, sems):
        copy.wait()


def finish(meta, parts):
    wide = parts[0].shape[1]
    return pl.pallas_call(
        finish_kernel,
        out_shape=shaped((2 * TILE, N_HEAD * wide)),
        in_specs=[SMEM] + [HBM] * len(parts),
        out_specs=VMEM,
        scratch_shapes=[pltpu.SemaphoreType.DMA((len(parts),))],
        compiler_params=params(8),
        cost_estimate=cost(0, 4 * 2 * TILE * N_HEAD * wide),
        name="finish",
    )(meta, *parts)


def rows_to(pairs):
    return [(a * ROW + j, b * ROW + j) for a, b in pairs for j in range(ROW)]


def over_row(x):
    groups = [[a * ROW + j for j in range(ROW)] for a in range(4)]
    return lax.all_to_all(
        x, "ctx", split_axis=0, concat_axis=0, tiled=True, axis_index_groups=groups
    )


def local(queries, key_rows, value_rows, block_gates):
    meta = jnp.stack([lax.axis_index("ctx"), lax.axis_index("head")]).astype(I32)
    q_parts = over_head([queries, *split(meta, 1, N_HEAD, (queries,))])
    table, place = plan(meta, block_gates.reshape(-1), lax.axis_size("ctx"))
    far, near, first = pack(meta, False, table, q_parts)
    (second,) = pack(meta, True, table, q_parts)
    first = over_row(first)
    far = lax.ppermute(far, "ctx", rows_to([(3, 0), (2, 1)]))
    near = lax.ppermute(near, "ctx", rows_to([(1, 0), (3, 2)]))
    kv_parts = over_head(split(meta, 0, N_HEAD, (key_rows, value_rows), near))
    kv = join(meta, kv_parts)
    kv_one = lax.ppermute(kv, "ctx", rows_to([(0, 1), (1, 2), (2, 3)]))
    kv_two = lax.ppermute(kv, "ctx", rows_to([(1, 3)]))
    second = over_row(insert(meta, second, far, near))
    (first,) = gate(meta, 0, first, (kv,))
    second, first = gate(meta, 1, second, (kv, kv_one, kv_two), first)
    second = over_row(second)
    out0, out1, log0, log1, first = own(meta, q_parts, kv, first)
    first = over_row(first)
    far, near = cut(second)
    far = lax.ppermute(far, "ctx", rows_to([(0, 3), (1, 2)]))
    near = lax.ppermute(near, "ctx", rows_to([(0, 1), (2, 3)]))
    backs = (second, first, far, near)
    done = []
    for half, owned in enumerate(((out0, log0), (out1, log1))):
        done += over_head(merge(half, meta, place, backs, *owned))
    return finish(meta, done)


def solution(mesh):
    return jax.shard_map(
        local,
        mesh=mesh,
        in_specs=(
            P(("ctx", "head"), None),
            P(("ctx", "head"), None),
            P(("ctx", "head"), None),
            P("ctx", "head", None),
        ),
        out_specs=P(("ctx", "head"), None),
        check_vma=False,
    )
```

```python
import math

import jax
import jax.numpy as jnp
from jax import lax
from jax.experimental import pallas as pl
from jax.experimental.pallas import tpu as pltpu
from jax.sharding import PartitionSpec as P

HEAD_DIM = 128
TILE = 128
CAP = 2
N_HEAD = 4
ROW = 16
R = TILE
SLOTS = 5
EXTRA = 16
SEND = (2 * R + EXTRA, 3 * R + EXTRA)
LOG_AT = 2 * R
FAR = 2 * R + EXTRA
NEAR = EXTRA + R
FIRST = SEND[1]
FAR_AT = FIRST + SEND[0]
NEAR_AT = FAR_AT + FAR
UNUSED = NEAR_AT + NEAR
SCALE = HEAD_DIM**-0.5
SCALE2 = SCALE * math.log2(math.e)
NEG = -1e30
F32 = jnp.float32
BF16 = jnp.bfloat16
I32 = jnp.int32

SMEM = pl.BlockSpec(memory_space=pltpu.SMEM)
VMEM = pl.BlockSpec(memory_space=pltpu.VMEM)
HBM = pl.BlockSpec(memory_space=pltpu.HBM)


def params(mib):
    return pltpu.CompilerParams(vmem_limit_bytes=mib * 2**20)


def cost(flops, data, exps=0):
    return pl.CostEstimate(flops=flops, bytes_accessed=data, transcendentals=exps)


def shaped(shape, kind=BF16):
    return jax.ShapeDtypeStruct(shape, kind)


def run_copies(pairs, sems):
    copies = [pltpu.make_async_copy(a, b, sems.at[i]) for i, (a, b) in enumerate(pairs)]
    for copy in copies:
        copy.start()
    return copies


def plan_kernel(meta, gates, table, place):
    me = meta[0] // ROW

    def clear(i, _):
        table[2 * i] = -1
        table[2 * i + 1] = -1
        return 0

    def note(pair, k):
        e = 3 * pair + k
        b = gates[e]
        place[e] = UNUSED // 16 * 1024 + 32 * 16

        @pl.when(b >= 0)
        def _():
            rank = (table[2 * b] >= 0).astype(I32)
            table[2 * b + rank] = pair
            target = lax.shift_right_logical(b, 4)
            away = me - target
            far = jnp.logical_and(me >= 2, target == 0)
            four = jnp.logical_or(
                jnp.logical_and(me == 1, away == 1), jnp.logical_and(me == 3, away == 2)
            )
            row = jnp.where(away == 0, FIRST, jnp.where(far, FAR_AT, 0)) + rank * R
            row = jnp.where(four, EXTRA + jnp.where(rank == 0, LOG_AT, NEAR_AT), row)
            slot = jnp.where(away == 0, 8, jnp.where(far, 18, 2)) + rank
            slot = jnp.where(four, 4 + 24 * rank, slot)
            place[e] = row * 64 + slot * 16 + jnp.bitwise_and(b, 15)

    def notes(pair, _):
        for k in range(3):
            note(pair, k)
        return 0

    lax.fori_loop(0, table.shape[0] // 2, clear, 0)
    lax.fori_loop(0, gates.shape[0] // 3, notes, 0)


def plan(meta, gates, blocks):
    return pl.pallas_call(
        plan_kernel,
        out_shape=(shaped((blocks * CAP,), I32), shaped(gates.shape, I32)),
        in_specs=[SMEM, SMEM],
        out_specs=(SMEM, SMEM),
        compiler_params=params(4),
        name="plan",
    )(meta, gates)


def split_kernel(count, first, parts, meta, *refs):
    ins, outs = refs[:count], refs[-2 - 2 * parts : -2 - parts]
    boxes, (reads, saves) = refs[-2 - parts : -2], refs[-2:]
    loads = []
    for i, box in enumerate(boxes):
        g = lax.rem(meta[1] + first + i, N_HEAD)
        at, pairs = 0, []
        for ref in ins:
            wide = ref.shape[1] // N_HEAD
            cols = pl.ds(pl.multiple_of(g * wide, 128), wide)
            pairs.append((ref.at[:, cols], box.at[:, pl.ds(at, wide)]))
            at += wide
        loads.append(run_copies(pairs, reads.at[i]))
    done = []
    for i, load in enumerate(loads):
        for copy in load:
            copy.wait()
        done.append(pltpu.make_async_copy(boxes[i], outs[i], saves.at[i]))
        done[-1].start()
    for copy in done:
        copy.wait()


def split(meta, first, end, ins, *earlier):
    rows, wide = ins[0].shape[0], sum(x.shape[1] for x in ins) // N_HEAD
    parts = end - first

    def kernel(*refs):
        split_kernel(len(ins), first, parts, *refs)

    return pl.pallas_call(
        kernel,
        out_shape=[shaped((rows, wide))] * parts,
        in_specs=[SMEM] + [HBM] * (len(ins) + len(earlier)),
        out_specs=[HBM] * parts,
        scratch_shapes=[pltpu.VMEM((rows, wide), BF16)] * parts
        + [
            pltpu.SemaphoreType.DMA((parts, len(ins))),
            pltpu.SemaphoreType.DMA((parts,)),
        ],
        compiler_params=params(8 if earlier else 56),
        cost_estimate=cost(0, 4 * rows * wide * parts),
        name="split",
    )(meta, *ins, *earlier)


def over_head(parts):
    got = [parts[0]]
    for step in range(1, N_HEAD):
        pairs = [(y, (y + step) % N_HEAD) for y in range(N_HEAD)]
        got.append(lax.ppermute(parts[step], "head", pairs))
    return got


def by_source(y, refs, whole):
    size = refs[0].shape[0]
    pairs = []
    if refs[0].shape[1] != whole.shape[1]:
        wide = whole.shape[1]
        own = refs[0].at[:, pl.ds(pl.multiple_of(y * wide, 128), wide)]
        refs = (own,) + tuple(refs[1:])
    for step, ref in enumerate(refs):
        source = lax.rem(y - step + N_HEAD, N_HEAD)
        pairs.append((ref, whole.at[pl.ds(pl.multiple_of(source * size, 16), size)]))
    return pairs


def join_kernel(meta, *refs):
    pieces, whole, sems = refs[:N_HEAD], refs[N_HEAD], refs[N_HEAD + 1]
    for copy in run_copies(by_source(meta[1], pieces, whole), sems):
        copy.wait()


def join(meta, pieces):
    rows, cols = pieces[0].shape
    return pl.pallas_call(
        join_kernel,
        out_shape=shaped((N_HEAD * rows, cols)),
        in_specs=[SMEM] + [HBM] * N_HEAD,
        out_specs=VMEM,
        scratch_shapes=[pltpu.SemaphoreType.DMA((N_HEAD,))],
        compiler_params=params(6),
        cost_estimate=cost(0, 4 * N_HEAD * rows * cols),
        name="join",
    )(meta, *pieces)


def pack_kernel(late, meta, table, q0, q1, q2, q3, *refs):
    count = (len(refs) - 2) // 2
    outs, boxes, q_all, sems = refs[:count], refs[count : 2 * count], refs[-2], refs[-1]
    me = meta[0] // ROW
    for copy in run_copies(by_source(meta[1], (q0, q1, q2, q3), q_all), sems):
        copy.wait()
    lane = lax.broadcasted_iota(I32, (EXTRA, 128), 1)

    def entry(j, target, rank):
        return table[2 * (jnp.maximum(target, 0) * ROW + j) + rank]

    def fill(into, j, row, target, rank):
        e = jnp.maximum(entry(j, target, rank), 0)
        tile = lax.shift_right_logical(e, 3)
        head = jnp.bitwise_and(e, 7)
        into[j, row : row + R, :] = q_all[
            pl.ds(pl.multiple_of(tile * R, R), R),
            pl.ds(pl.multiple_of(head * HEAD_DIM, HEAD_DIM), HEAD_DIM),
        ]

    def codes(j, *slots):
        marks = jnp.full((EXTRA, 128), -1, I32)
        for slot, target, rank in slots:
            e = entry(j, target, rank)
            kv_head = jnp.bitwise_and(lax.shift_right_logical(e, 2), 1)
            code = jnp.where(jnp.logical_and(target >= 0, e >= 0), kv_head, -1)
            marks = jnp.where(lane == slot, code, marks)
        return marks.astype(F32).astype(BF16)

    split_row = jnp.where(me == 3, 1, me - 1)

    def own_row(j, _):
        z1 = boxes[2]
        fill(z1, j, 0, me, 0)
        fill(z1, j, R, me, 1)
        z1[j, 2 * R :, :] = codes(j, (0, me, 0), (1, me, 1))
        return 0

    def moved(j, _):
        far, near = boxes[:2]
        fill(far, j, 0, 0, 0)
        fill(far, j, R, 0, 1)
        far[j, 2 * R :, :] = codes(j, (2, 0, 0), (3, 0, 1))
        fill(near, j, 0, split_row, 1)
        near[j, R:, :] = codes(j, (4, split_row, 1))
        return 0

    def other_rows(j, _):
        z2 = boxes[0]
        fill(z2, j, 0, me - 1, 0)
        fill(z2, j, R, me - 1, 1)
        fill(z2, j, 2 * R, split_row, 0)
        z2[j, 3 * R :, :] = codes(j, (2, me - 1, 0), (3, me - 1, 1), (4, split_row, 0))
        return 0

    saves = []
    works = ((other_rows, (0,)),) if late else ((moved, (0, 1)), (own_row, (2,)))
    for work, group in works:
        lax.fori_loop(0, ROW, work, 0, unroll=2)
        for i in group:
            saves.append(pltpu.make_async_copy(boxes[i], outs[i], sems.at[N_HEAD + i]))
            saves[-1].start()
    for save in saves:
        save.wait()


def pack(meta, late, table, q_parts):
    rows, wide = q_parts[1].shape
    sizes = (SEND[1],) if late else (FAR, NEAR, SEND[0])

    def kernel(*refs):
        pack_kernel(late, *refs)

    return pl.pallas_call(
        kernel,
        out_shape=[shaped((ROW, size, HEAD_DIM)) for size in sizes],
        in_specs=[SMEM, SMEM] + [HBM] * N_HEAD,
        out_specs=[HBM] * len(sizes),
        scratch_shapes=[pltpu.VMEM((ROW, size, HEAD_DIM), BF16) for size in sizes]
        + [
            pltpu.VMEM((N_HEAD * rows, wide), BF16),
            pltpu.SemaphoreType.DMA((N_HEAD + len(sizes),)),
        ],
        compiler_params=params(8 if late else 56),
        cost_estimate=cost(0, 2 * (N_HEAD * rows * wide + ROW * sum(sizes) * HEAD_DIM)),
        name="pack",
    )(meta, table, *q_parts)


def insert_kernel(meta, z_in, far, near, *refs):
    z, box, marks, sems = refs[-4:]
    me = meta[0] // ROW
    two, four, last = pl.ds(0, 2 * R), pl.ds(2 * R, R), pl.ds(3 * R, EXTRA)
    has_far, has_near = me <= 1, jnp.logical_or(me == 0, me == 2)
    reads = (
        (jnp.logical_not(has_far), z_in.at[:, two], box.at[:, two], sems.at[0]),
        (has_far, far.at[:, two], box.at[:, two], sems.at[0]),
        (jnp.logical_not(has_near), z_in.at[:, four], box.at[:, four], sems.at[1]),
        (has_near, near.at[:, pl.ds(0, R)], box.at[:, four], sems.at[1]),
    )
    for cond, source, target, sem in reads:

        @pl.when(cond)
        def _(source=source, target=target, sem=sem):
            pltpu.make_async_copy(source, target, sem).start()

    loads = [
        pltpu.make_async_copy(source, marks.at[i], sems.at[2 + i])
        for i, source in enumerate(
            (z_in.at[:, last], far.at[:, pl.ds(2 * R, EXTRA)], near.at[:, pl.ds(R, EXTRA)])
        )
    ]
    for load in loads:
        load.start()
    for load in loads:
        load.wait()
    lane = lax.broadcasted_iota(I32, (EXTRA, 128), 1)
    from_far = jnp.logical_and(lane < 4, me <= 1)
    from_near = jnp.logical_and(lane == 4, lax.rem(me, 2) == 0)
    for j in range(ROW):
        mine, theirs, one = (marks[i, j].astype(F32) for i in range(3))
        mine = jnp.where(from_far, theirs, jnp.where(from_near, one, mine))
        box[j, 3 * R :, :] = mine.astype(BF16)
    saves = []
    for i, region in enumerate((two, four, last)):
        if i < 2:
            pltpu.make_async_copy(z_in.at[:, region], box.at[:, region], sems.at[i]).wait()
        saves.append(pltpu.make_async_copy(box.at[:, region], z.at[:, region], sems.at[5 + i]))
        saves[-1].start()
    for save in saves:
        save.wait()


def insert(meta, z, far, near, *earlier):
    return pl.pallas_call(
        insert_kernel,
        out_shape=shaped(z.shape),
        in_specs=[SMEM] + [HBM] * (3 + len(earlier)),
        out_specs=HBM,
        scratch_shapes=[
            pltpu.VMEM(z.shape, BF16),
            pltpu.VMEM((3, ROW, EXTRA, 128), BF16),
            pltpu.SemaphoreType.DMA((8,)),
        ],
        compiler_params=params(8),
        cost_estimate=cost(0, 4 * z.size),
        name="insert",
    )(meta, z, far, near, *earlier)


def cut_kernel(back, far, near, sems):
    pairs = [
        (back.at[:, pl.ds(0, FAR)], far),
        (back.at[:, pl.ds(LOG_AT, NEAR)], near),
    ]
    for copy in run_copies(pairs, sems):
        copy.wait()


def cut(back):
    return pl.pallas_call(
        cut_kernel,
        out_shape=(shaped((ROW, FAR, HEAD_DIM)), shaped((ROW, NEAR, HEAD_DIM))),
        in_specs=[HBM],
        out_specs=(VMEM, VMEM),
        scratch_shapes=[pltpu.SemaphoreType.DMA((2,))],
        compiler_params=params(6),
        cost_estimate=cost(0, 4 * ROW * (FAR + NEAR) * HEAD_DIM),
        name="cut",
    )(back)


def dot_t(a, b):
    return lax.dot_general(a, b, (((1,), (1,)), ((), ())), preferred_element_type=F32)


def dot(a, b):
    return lax.dot_general(a, b, (((1,), (0,)), ((), ())), preferred_element_type=F32)


def to_row(log):
    lane = lax.broadcasted_iota(I32, (R, R), 1)
    row = lax.broadcasted_iota(I32, (R, R), 0)
    wide = jnp.broadcast_to(log, (R, R))
    return jnp.sum(jnp.where(lane == row, wide, 0.0), axis=0, keepdims=True)


def attend(scores, values):
    top = jnp.max(scores, axis=-1, keepdims=True)
    weights = jnp.exp2((scores - top) * SCALE2)
    total = jnp.sum(weights, axis=-1, keepdims=True)
    mixed = dot(weights.astype(BF16), values) / total
    return mixed, top * SCALE + jnp.log(total)


def gate_kernel(part, meta, *refs):
    n_kv = 3 if part else 1
    z_in, kvs, out_ref = refs[0], refs[1 : 1 + n_kv], refs[1 + n_kv]
    z, out, kv, logs, codes, lists, counts, marks, sems, kv_sems, out_sems = refs[2 + n_kv :]
    me = meta[0] // ROW
    groups = ((2, 3), (4,)) if part else ((0, 1),)
    size = SEND[part]
    known = pltpu.make_async_copy(
        z_in.at[:, pl.ds(size - EXTRA, EXTRA)], z.at[:, pl.ds(size - EXTRA, EXTRA)], sems.at[0]
    )
    known.start()
    loads = []
    for group in range(len(groups)):
        rows = pl.ds(2 * R * group, R * len(groups[group]))
        loads.append(pltpu.make_async_copy(z_in.at[:, rows], z.at[:, rows], sems.at[1 + group]))
        loads[-1].start()
        if part:
            stores = (me == 0, me > 0, False) if group == 0 else (
                me == 0, jnp.logical_or(me == 1, me == 2), me == 3
            )
            for i, chosen in enumerate(stores):
                if chosen is not False:

                    @pl.when(chosen)
                    def _(i=i, group=group):
                        pltpu.make_async_copy(kvs[i], kv.at[group], kv_sems.at[group]).start()
        else:
            pltpu.make_async_copy(kvs[0], kv.at[0], kv_sems.at[0]).start()
    known.wait()
    for j in range(ROW):
        marks[j : j + 1, :] = z[j, size - EXTRA :, :].astype(F32)[:1].astype(I32)
    known = pltpu.make_async_copy(marks, codes, sems.at[0])
    known.start()
    known.wait()
    for i in range(2 * len(groups)):
        counts[i] = 0

    def scan(j, _):
        for group, slots in enumerate(groups):
            for slot in slots:
                code = codes[j, slot]

                @pl.when(code >= 0)
                def _(group=group, slot=slot, code=code):
                    i = 2 * group + code
                    n = counts[i]
                    lists[i, n] = j * 8 + slot
                    counts[i] = n + 1

        return 0

    lax.fori_loop(0, ROW, scan, 0)
    saves = []

    def save(first, rows):
        region = pl.ds(first, rows)
        copy = pltpu.make_async_copy(
            out.at[:, region], out_ref.at[:, region], out_sems.at[len(saves)]
        )
        copy.start()
        saves.append(copy)

    for i in range(2 * len(groups)):
        group, kv_head = i // 2, i % 2
        count = counts[i]
        if kv_head == 0:
            loads[group].wait()
            pltpu.make_async_copy(kvs[0], kv.at[group], kv_sems.at[group]).wait()

        def batch(first, width, i=i, group=group, kv_head=kv_head, count=count):
            keys = kv[group, :, kv_head * HEAD_DIM : (kv_head + 1) * HEAD_DIM]
            values = kv[group, :, (2 + kv_head) * HEAD_DIM : (3 + kv_head) * HEAD_DIM]
            where, scores = [], []
            for u in range(width):
                item = lists[i, jnp.minimum(first + u, count - 1)]
                where.append((lax.shift_right_logical(item, 3), jnp.bitwise_and(item, 7)))
            for u in range(0, width, 2):
                q = [
                    z[j, pl.ds(pl.multiple_of((s - 2 * part) * R, R), R), :]
                    for j, s in where[u : u + 2]
                ]
                scores.append(dot_t(jnp.concatenate(q, axis=0), keys))
            done = [attend(x, values) for x in scores]
            for u, (j, s) in enumerate(where):
                mixed, log = done[u // 2]
                rows = slice(u % 2 * R, (u % 2 + 1) * R)
                at = (s - 2 * part) * R + jnp.where(s >= 4, EXTRA, 0)
                out[j, pl.ds(pl.multiple_of(at, 16), R), :] = mixed[rows].astype(BF16)
                log = to_row(log[rows])
                high = log.astype(BF16).astype(F32)
                logs[j, pl.ds(s, 1), :] = high
                logs[j, pl.ds(8 + s, 1), :] = log - high

        eights = lax.shift_right_logical(count, 3)
        rest = count - 8 * eights
        fours = lax.shift_right_logical(rest + 1, 2)

        def eight(n, _, batch=batch):
            batch(8 * n, 8)
            return 0

        def four(n, _, batch=batch, eights=eights):
            batch(8 * eights + 4 * n, 4)
            return 0

        lax.fori_loop(0, eights, eight, 0)
        lax.fori_loop(0, fours, four, 0)

        @pl.when(rest > 4 * fours)
        def _(batch=batch, eights=eights, fours=fours):
            batch(8 * eights + 4 * fours, 2)

        if i == 1:
            save(0, 2 * R)
    for j in range(ROW):
        out[j, LOG_AT : LOG_AT + EXTRA, :] = logs[j].astype(BF16)
    save(LOG_AT, size - 2 * R)
    for copy in saves:
        copy.wait()


def gate(meta, part, z, kvs, *held):
    keys = kvs[0].shape[0]
    items = ROW * (2 + part)
    n_kv = len(kvs)

    def kernel(*refs):
        ins = 2 + n_kv + len(held)
        gate_kernel(part, *refs[: 2 + n_kv], refs[ins], *refs[ins + 1 + len(held) :])

    return pl.pallas_call(
        kernel,
        out_shape=[shaped((ROW, SEND[part], HEAD_DIM))] + [shaped(x.shape) for x in held],
        in_specs=[SMEM, HBM] + [HBM] * (n_kv + len(held)),
        out_specs=[HBM] * (1 + len(held)),
        input_output_aliases={2 + n_kv + i: 1 + i for i in range(len(held))},
        scratch_shapes=[
            pltpu.VMEM((ROW, SEND[part], HEAD_DIM), BF16),
            pltpu.VMEM((ROW, SEND[part], HEAD_DIM), BF16),
            pltpu.VMEM((1 + part,) + kvs[0].shape, BF16),
            pltpu.VMEM((ROW, 16, 128), F32),
            pltpu.SMEM((ROW, 128), I32),
            pltpu.SMEM((4, ROW * CAP), I32),
            pltpu.SMEM((8,), I32),
            pltpu.VMEM((ROW, 128), I32),
            pltpu.SemaphoreType.DMA((3,)),
            pltpu.SemaphoreType.DMA((2,)),
            pltpu.SemaphoreType.DMA((2,)),
        ],
        compiler_params=params(56),
        cost_estimate=cost(4 * items * R * keys * HEAD_DIM, 8 * 2**20, items * R * keys),
        name="gate",
    )(meta, z, *kvs, *held)


def own_kernel(meta, q0, q1, q2, q3, kv, _, out0, out1, log0, log1, __, q_all, sems):
    for copy in run_copies(by_source(meta[1], (q0, q1, q2, q3), q_all), sems):
        copy.wait()
    tiles = q_all.shape[0] // R
    heads = q_all.shape[1] // HEAD_DIM
    row = lax.rem(lax.broadcasted_iota(I32, (2 * R, TILE), 0), R)
    seen = row >= lax.broadcasted_iota(I32, (2 * R, TILE), 1)
    for tile in range(tiles):
        rows = slice(tile * R, (tile + 1) * R)
        past, now = slice(0, tile * TILE), slice(tile * TILE, (tile + 1) * TILE)
        out, logs = (out0, log0) if tile % 2 == 0 else (out1, log1)
        to = slice(tile // 2 * R, (tile // 2 + 1) * R)
        for pair in range(0, heads, 2):
            kv_head = pair // (heads // 2)
            q = jnp.concatenate(
                [q_all[rows, h * HEAD_DIM : (h + 1) * HEAD_DIM] for h in (pair, pair + 1)], axis=0
            )
            k_col = slice(kv_head * HEAD_DIM, (kv_head + 1) * HEAD_DIM)
            v_col = slice((2 + kv_head) * HEAD_DIM, (3 + kv_head) * HEAD_DIM)
            near = jnp.where(seen, dot_t(q, kv[now, k_col]), NEG)
            top = jnp.max(near, axis=-1, keepdims=True)
            if tile:
                far = dot_t(q, kv[past, k_col])
                top = jnp.maximum(top, jnp.max(far, axis=-1, keepdims=True))
            near = jnp.exp2((near - top) * SCALE2)
            total = jnp.sum(near, axis=-1, keepdims=True)
            mixed = dot(near.astype(BF16), kv[now, v_col])
            if tile:
                far = jnp.exp2((far - top) * SCALE2)
                total = total + jnp.sum(far, axis=-1, keepdims=True)
                mixed = mixed + dot(far.astype(BF16), kv[past, v_col])
            mixed = mixed / total
            log = top * SCALE + jnp.log(total)
            for u in range(2):
                head = pair + u
                out[to, head * HEAD_DIM : (head + 1) * HEAD_DIM] = mixed[u * R : (u + 1) * R]
                at = tile // 2 * heads + head
                logs[at : at + 1, :] = to_row(log[u * R : (u + 1) * R])


def own(meta, q_parts, kv, held):
    rows, wide = q_parts[1].shape
    rows = N_HEAD * rows
    units = rows * wide // HEAD_DIM
    out, logs = shaped((rows // 2, wide), F32), shaped((units // R // 2, 128), F32)
    return pl.pallas_call(
        own_kernel,
        out_shape=(out, out, logs, logs, shaped(held.shape)),
        in_specs=[SMEM] + [HBM] * N_HEAD + [VMEM, HBM],
        out_specs=(VMEM, VMEM, VMEM, VMEM, HBM),
        input_output_aliases={2 + N_HEAD: 4},
        scratch_shapes=[pltpu.VMEM((rows, wide), BF16), pltpu.SemaphoreType.DMA((N_HEAD,))],
        compiler_params=params(56),
        cost_estimate=cost(4 * units * 640 * HEAD_DIM, 8 * 2**20, units * 640),
        name="own",
    )(meta, *q_parts, kv, held)


def merge_kernel(
    half, meta, place, far_back, z_back, farb, nearb, own_ref, own_log,
    o0, o1, o2, o3, items, logs, got, done, sems
):
    y = meta[1]
    copies = run_copies(
        [
            (far_back, items.at[:, pl.ds(0, SEND[1])]),
            (z_back, items.at[:, pl.ds(FIRST, SEND[0])]),
            (farb, items.at[:, pl.ds(FAR_AT, FAR)]),
            (nearb, items.at[:, pl.ds(NEAR_AT, NEAR)]),
        ],
        sems,
    )
    heads = own_ref.shape[1] // HEAD_DIM
    items[0, UNUSED : UNUSED + R, :] = jnp.zeros((R, HEAD_DIM), BF16)
    logs[0, 32:40, :] = jnp.full((8, 128), NEG, F32)
    for copy in copies:
        copy.wait()
    for j in range(ROW):
        for group, at in enumerate((LOG_AT, FIRST + LOG_AT, FAR_AT + LOG_AT, NEAR_AT)):
            halves = items[j, at : at + EXTRA, :].astype(F32)
            logs[j, 8 * group : 8 * group + 8, :] = halves[:8] + halves[8:]

    def each(pair, _):
        rows = pl.ds(pl.multiple_of(pair * R, R), R)
        where = {}
        for head in range(heads):
            for k in range(3):
                at = place[((2 * pair + half) * heads + head) * 3 + k]
                row = lax.shift_right_logical(at, 10) * 16
                slot = jnp.bitwise_and(lax.shift_right_logical(at, 4), 63)
                j = jnp.bitwise_and(at, 15)
                where[head, k] = (j, row)
                got[k * heads + head : k * heads + head + 1, :] = logs[j, pl.ds(slot, 1), :]
        first = own_log[pl.ds(pl.multiple_of(pair * heads, heads), heads), :]
        others = [got[k * heads : (k + 1) * heads, :] for k in range(3)]
        top = first
        for other in others:
            top = jnp.maximum(top, other)
        weights = [jnp.exp(x - top) for x in [first] + others]
        total = weights[0] + weights[1] + weights[2] + weights[3]
        shares = jnp.concatenate([w / total for w in weights], axis=0)
        shares = jnp.transpose(shares)
        for head in range(heads):
            cols = slice(head * HEAD_DIM, (head + 1) * HEAD_DIM)
            mixed = shares[:, head : head + 1] * own_ref[rows, cols]
            for k in range(3):
                j, row = where[head, k]
                item = items[j, pl.ds(pl.multiple_of(row, 16), R), :].astype(F32)
                at = (k + 1) * heads + head
                mixed = mixed + shares[:, at : at + 1] * item
            done[rows, cols] = mixed.astype(BF16)
        return 0

    lax.fori_loop(0, N_HEAD, each, 0, unroll=N_HEAD)
    pairs = []
    for step, ref in enumerate((o0, o1, o2, o3)):
        target = lax.rem(y + step, N_HEAD)
        pairs.append((done.at[pl.ds(pl.multiple_of(target * R, R), R)], ref))
    for copy in run_copies(pairs, sems):
        copy.wait()


def merge(half, meta, place, backs, own_out, own_log):
    rows, wide = own_out.shape

    def kernel(*refs):
        merge_kernel(half, *refs)

    return pl.pallas_call(
        kernel,
        out_shape=[shaped((R, wide))] * N_HEAD,
        in_specs=[SMEM, SMEM] + [HBM] * 4 + [VMEM] * 2,
        out_specs=[HBM] * N_HEAD,
        scratch_shapes=[
            pltpu.VMEM((ROW, UNUSED + R, HEAD_DIM), BF16),
            pltpu.VMEM((ROW, 40, 128), F32),
            pltpu.VMEM((24, 128), F32),
            pltpu.VMEM((rows, wide), BF16),
            pltpu.SemaphoreType.DMA((5,)),
        ],
        compiler_params=params(20),
        cost_estimate=cost(20 * rows * wide, 8 * 2**20),
        name="merge",
    )(meta, place, *backs, own_out, own_log)


def finish_kernel(meta, *refs):
    parts, out, sems = refs[:-2], refs[-2], refs[-1]
    y = meta[1]
    wide = parts[0].shape[1]
    pairs = []
    for half in range(2):
        for step in range(N_HEAD):
            source = lax.rem(y - step + N_HEAD, N_HEAD)
            cols = pl.ds(pl.multiple_of(source * wide, 128), wide)
            pairs.append((parts[half * N_HEAD + step], out.at[pl.ds(half * R, R), cols]))
    for copy in run_copies(pairs, sems):
        copy.wait()


def finish(meta, parts):
    wide = parts[0].shape[1]
    return pl.pallas_call(
        finish_kernel,
        out_shape=shaped((2 * TILE, N_HEAD * wide)),
        in_specs=[SMEM] + [HBM] * len(parts),
        out_specs=VMEM,
        scratch_shapes=[pltpu.SemaphoreType.DMA((len(parts),))],
        compiler_params=params(8),
        cost_estimate=cost(0, 4 * 2 * TILE * N_HEAD * wide),
        name="finish",
    )(meta, *parts)


def rows_to(pairs):
    return [(a * ROW + j, b * ROW + j) for a, b in pairs for j in range(ROW)]


def over_row(x):
    groups = [[a * ROW + j for j in range(ROW)] for a in range(4)]
    return lax.all_to_all(
        x, "ctx", split_axis=0, concat_axis=0, tiled=True, axis_index_groups=groups
    )


def local(queries, key_rows, value_rows, block_gates):
    meta = jnp.stack([lax.axis_index("ctx"), lax.axis_index("head")]).astype(I32)
    q_parts = over_head([queries, *split(meta, 1, N_HEAD, (queries,))])
    table, place = plan(meta, block_gates.reshape(-1), lax.axis_size("ctx"))
    far, near, first = pack(meta, False, table, q_parts)
    (second,) = pack(meta, True, table, q_parts)
    first = over_row(first)
    far = lax.ppermute(far, "ctx", rows_to([(3, 0), (2, 1)]))
    near = lax.ppermute(near, "ctx", rows_to([(1, 0), (3, 2)]))
    kv_parts = over_head(split(meta, 0, N_HEAD, (key_rows, value_rows), near))
    kv = join(meta, kv_parts)
    kv_one = lax.ppermute(kv, "ctx", rows_to([(0, 1), (1, 2), (2, 3)]))
    kv_two = lax.ppermute(kv, "ctx", rows_to([(1, 3)]))
    second = over_row(insert(meta, second, far, near))
    (first,) = gate(meta, 0, first, (kv,))
    second, first = gate(meta, 1, second, (kv, kv_one, kv_two), first)
    second = over_row(second)
    out0, out1, log0, log1, first = own(meta, q_parts, kv, first)
    first = over_row(first)
    far, near = cut(second)
    far = lax.ppermute(far, "ctx", rows_to([(0, 3), (1, 2)]))
    near = lax.ppermute(near, "ctx", rows_to([(0, 1), (2, 3)]))
    backs = (second, first, far, near)
    done = []
    for half, owned in enumerate(((out0, log0), (out1, log1))):
        done += over_head(merge(half, meta, place, backs, *owned))
    return finish(meta, done)


def solution(mesh):
    return jax.shard_map(
        local,
        mesh=mesh,
        in_specs=(
            P(("ctx", "head"), None),
            P(("ctx", "head"), None),
            P(("ctx", "head"), None),
            P("ctx", "head", None),
        ),
        out_specs=P(("ctx", "head"), None),
        check_vma=False,
    )
```
